256 devices in a mesh: dp: 8 (over y, core), seq: 32 (over x, z).
Axes of the slice: x: 4, y: 4, z: 8, core: 2. Of those that a mesh axis runs over, the one named last changes fastest.
Arguments:
- queries: bfloat16 [8, 16384, 640], P('dp', 'seq'), may hold values from -10 to 10
- keys: bfloat16 [8, 16384, 640], P('dp', 'seq'), may hold values from -4 to 4
- values: bfloat16 [8, 16384, 640], P('dp', 'seq'), may hold values from -6 to 6
- upstream: bfloat16 [8, 16384, 1280], P('dp', 'seq'), may hold values from -24 to 24
- out_weight: bfloat16 [640, 1280], replicated, may hold values from -0.25 to 0.25
- visible: int32 [8, 16384], P('dp', 'seq'), may hold values from 0 to 1, as said below
Outputs:
- grad_queries: bfloat16 [8, 16384, 640], P('dp', 'seq')
- grad_keys: bfloat16 [8, 16384, 640], P('dp', 'seq')
- grad_values: bfloat16 [8, 16384, 640], P('dp', 'seq')
- grad_weight: float32 [640, 1280], P('seq')
The draws below stay inside these ranges and needn't reach their ends.
Inputs may be any that keep to these rules, and one draw needn't show every extreme that they name: In every scene, the patches of the devices 2 j and 2 j + 1 along seq (512 each, in order) hold together at most 144 visible ones; in every scene one device's patches hold exactly 144 visible ones and those of its partner none.
All inputs are finite; a program needn't handle non-finite values.
Results may differ from the reference program's by a relative error of at most 0.014.
Values may be sent and summed in bfloat16 or wider, within the bound.
A program may use at most 128 MiB of HBM per device.

```python
import jax
import jax.numpy as jnp
from jax import lax

D = 1280
HEADS = 8
HEAD_DIM = 80
HD = 640
ROWS = 512
VIS_MAX = 144
L = 16384
SCENES = 8
N_SEQ = 32


def draw_queries(key, part):
    own_key = jax.random.fold_in(key, 31)
    result = jnp.clip(jax.random.normal(own_key, (SCENES, L, HD), jnp.float32), -4.0, 4.0)
    return result.astype(jnp.bfloat16)


def draw_keys(key, part):
    own_key = jax.random.fold_in(key, 37)
    result = jnp.clip(jax.random.normal(own_key, (SCENES, L, HD), jnp.float32), -4.0, 4.0)
    return result.astype(jnp.bfloat16)


def draw_visible(key, part):
    key = jax.random.fold_in(key, 11)
    first_key, second_key, pick_key, flip_key, order_key = jax.random.split(key, 5)
    per_scene = L // ROWS
    pair_count = SCENES * per_scene // 2
    first = jax.random.randint(first_key, (pair_count,), 0, VIS_MAX + 1)
    second = jax.random.randint(second_key, (pair_count,), 0, VIS_MAX + 1) % (VIS_MAX + 1 - first)
    chosen = jax.random.randint(pick_key, (SCENES, 1), 0, per_scene // 2)
    forced = (jnp.arange(per_scene // 2)[None, :] == chosen).reshape(pair_count)
    first = jnp.where(forced, VIS_MAX, first)
    second = jnp.where(forced, 0, second)
    flipped = jax.random.randint(flip_key, (pair_count,), 0, 2) == 1
    left_count = jnp.where(flipped, second, first)
    right_count = jnp.where(flipped, first, second)
    counts = jnp.stack([left_count, right_count], axis=1).reshape(SCENES * per_scene)
    block_keys = jax.random.split(order_key, SCENES * per_scene)
    ranks = jax.vmap(lambda block_key: jax.random.permutation(block_key, ROWS))(block_keys)
    return (ranks < counts[:, None]).astype(jnp.int32).reshape(SCENES, L)


def block_levels(key, extent, cuts, smallest, top_value):
    loudness = 1.0
    for axis_at, blocks in cuts:
        draws = jax.random.uniform(jax.random.fold_in(jax.random.fold_in(key, 6), axis_at), (blocks,), jnp.float32, smallest / len(cuts), top_value / len(cuts))
        loudness = loudness * jnp.repeat(jnp.exp(draws), extent[axis_at] // blocks).reshape((-1,) + (1,) * (len(extent) - 1 - axis_at))
    return loudness


def gaussian(key, dims, width, most, cuts=(), kind=jnp.bfloat16):
    values = width * jax.random.normal(key, dims, jnp.float32)
    if cuts:
        values = values * block_levels(key, dims, cuts, -0.22, 0.18)
    return jnp.clip(values, -most, most).astype(kind)


def setup_inputs(seed: int = 0) -> dict:
    key_of = jax.random.split(jax.random.key(seed), 7)
    return {
        "queries": draw_queries(jax.random.fold_in(key_of[6], 71), 0),
        "keys": draw_keys(jax.random.fold_in(key_of[6], 71), 0),
        "values": gaussian(key_of[2], (SCENES, L, HD), 1.0, 6.0, ((0, 8), (1, 32))),
        "upstream": gaussian(key_of[3], (SCENES, L, D), 4.0, 24.0, ((0, 8), (1, 32))),
        "out_weight": gaussian(key_of[4], (HD, D), HD ** -0.5, 0.25),
        "visible": draw_visible(jax.random.fold_in(key_of[6], 71), 0),
    }


NEGATIVE_FILL = -1e30


def split_heads(matrix):
    return matrix.reshape(matrix.shape[0], HEADS, HEAD_DIM).transpose(1, 0, 2)


def merge_heads(stacked):
    return stacked.transpose(1, 0, 2).reshape(stacked.shape[1], HEADS * HEAD_DIM)


def head_grads(query_head, key_head, value_head, grad_head, key_live):
    score_scale = HEAD_DIM ** -0.5
    scores = jnp.dot(query_head, key_head.T, preferred_element_type=jnp.float32) * score_scale
    scores = jnp.where(key_live[None, :], scores, NEGATIVE_FILL)
    row_max = jnp.max(scores, axis=1, keepdims=True)
    log_total = row_max + jnp.log(jnp.sum(jnp.exp(scores - row_max), axis=1, keepdims=True))
    probability = jnp.exp(scores - log_total)
    weights = probability.astype(jnp.bfloat16)
    attended = jnp.dot(weights, value_head, preferred_element_type=jnp.float32).astype(jnp.bfloat16)
    row_delta = jnp.sum(grad_head.astype(jnp.float32) * attended.astype(jnp.float32), axis=1, keepdims=True)
    grad_prob = jnp.dot(grad_head, value_head.T, preferred_element_type=jnp.float32)
    grad_score = (probability * (grad_prob - row_delta) * score_scale).astype(jnp.bfloat16)
    grad_query = jnp.dot(grad_score, key_head, preferred_element_type=jnp.float32).astype(jnp.bfloat16)
    grad_key = jnp.dot(grad_score.T, query_head, preferred_element_type=jnp.float32).astype(jnp.bfloat16)
    grad_value = jnp.dot(weights.T, grad_head, preferred_element_type=jnp.float32).astype(jnp.bfloat16)
    return attended, grad_query, grad_key, grad_value


def scene_grads(queries, keys, values, upstream, visible, out_weight):
    capacity = N_SEQ * (VIS_MAX // 2)
    row_order = jnp.argsort(1 - visible, stable=True).astype(jnp.int32)[:capacity]
    live_rows = jnp.take(visible, row_order) == 1

    def pick_rows(source):
        taken = jnp.take(source, row_order, axis=0)
        return jnp.where(live_rows[:, None], taken, jnp.zeros_like(taken))

    query_rows = pick_rows(queries)
    key_rows = pick_rows(keys)
    value_rows = pick_rows(values)
    upstream_rows = pick_rows(upstream)
    grad_out = jnp.dot(upstream_rows, out_weight.T, preferred_element_type=jnp.float32).astype(jnp.bfloat16)

    def one_head(parts):
        return head_grads(parts[0], parts[1], parts[2], parts[3], live_rows)

    attended, grad_query, grad_key, grad_value = lax.map(
        one_head, (split_heads(query_rows), split_heads(key_rows), split_heads(value_rows), split_heads(grad_out)))
    attended = merge_heads(attended)
    weight_part = jnp.dot(attended.T, upstream_rows, preferred_element_type=jnp.float32)

    def place_back(grad_rows):
        merged = merge_heads(grad_rows)
        kept = jnp.where(live_rows[:, None], merged, jnp.zeros_like(merged))
        return jnp.zeros((visible.shape[0], kept.shape[1]), kept.dtype).at[row_order].set(kept)

    return place_back(grad_query), place_back(grad_key), place_back(grad_value), weight_part


def reference(queries, keys, values, upstream, out_weight, visible):
    def one_scene(parts):
        return scene_grads(parts[0], parts[1], parts[2], parts[3], parts[4], out_weight)

    grad_queries, grad_keys, grad_values, weight_parts = lax.map(
        one_scene, (queries, keys, values, upstream, visible))
    return grad_queries, grad_keys, grad_values, jnp.sum(weight_parts, axis=0)
```

```python
import functools

import jax
import jax.numpy as jnp
from jax import lax
from jax.experimental import pallas as pl
from jax.experimental.pallas import tpu as pltpu
from jax.sharding import PartitionSpec as P

HEAD_DIM = 80
VIS_MAX = 144
Z_RING = 8
Y_RING = 4

BF16 = jnp.bfloat16
F32 = jnp.float32
MESH = pl.DeviceIdType.MESH
FAR = 1e30


def nn(a, b):
    return jnp.dot(a, b, preferred_element_type=F32)


def nt(a, b):
    return lax.dot_general(a, b, (((1,), (1,)), ((), ())), preferred_element_type=F32)


def identity(n):
    rows = lax.broadcasted_iota(jnp.int32, (n, n), 0)
    cols = lax.broadcasted_iota(jnp.int32, (n, n), 1)
    return jnp.where(rows == cols, 1.0, 0.0).astype(BF16)


def lane_iota(rows, lanes):
    return lax.broadcasted_iota(jnp.int32, (rows, lanes), 1)


class Sizes:
    def __init__(self, nx, nz, ny, rows, cap, heads, width):
        self.nx, self.nz, self.ny = nx, nz, ny
        self.rows, self.cap, self.heads, self.width = rows, cap, heads, width
        self.pairs = nz // 2
        self.queries = self.pairs * cap
        self.keys = nx * self.queries
        self.block = 256 if self.keys % 256 == 0 else 128
        self.hd = heads * HEAD_DIM
        self.col_tiles = width // 128
        self.tiles = (HEAD_DIM // 16) * self.col_tiles
        self.share = -(-self.tiles // nz)
        self.out_rows = self.hd // (nx * nz)
        self.per_head = HEAD_DIM // self.out_rows


def kernel(
    sz,
    vis_ref, q_hbm, k_hbm, v_hbm, u_hbm, w_hbm,
    gq_hbm, gk_hbm, gv_hbm, gw_ref,
    qin, kin, vin, uin, win,
    send_a, recv_a, send_b, recv_b,
    kv, kvt, q_mask, q_zero, d_out, scores,
    send_e, recv_e, dkv, recv_c, send_d, recv_d,
    upk, wown, wsend1, wrecv1, wsend2, wrecv2, red, tiles, wrecv3, wsend4, wrecv4, wsend5, wrecv5,
    full, stage,
    load_sem, store_sem,
    a_s, a_r, b_s, b_r, g_s, g_r, e_s, e_r, c_s, c_r, d_s, d_r,
    w1_s, w1_r, w2_s, w2_r, w3_s, w3_r, w4_s, w4_r, w5_s, w5_r, w6_s, w6_r,
):
    nx, nz, ny, cap, heads = sz.nx, sz.nz, sz.ny, sz.cap, sz.heads
    nq, nk, blk, width = sz.queries, sz.keys, sz.block, sz.width
    scale = HEAD_DIM ** -0.5
    dp = lax.axis_index("dp")
    seq = lax.axis_index("seq")
    x, z = lax.div(seq, nz), lax.rem(seq, nz)
    y, core = lax.div(dp, 2), lax.rem(dp, 2)

    def z_peer(k):
        return lax.rem(z + k, nz)

    def x_peer(k):
        return lax.rem(x + k, nx)

    def at_z(k):
        return (dp, x * nz + z_peer(k))

    def at_x(k):
        return (dp, x_peer(k) * nz + z)

    def at_y(k):
        return (lax.rem(y + k, ny) * 2 + core, seq)

    def remote(src, dst, ss, rs, dev):
        return pltpu.make_async_remote_copy(
            src_ref=src, dst_ref=dst, send_sem=ss, recv_sem=rs, device_id=dev, device_id_type=MESH
        )

    barrier = pltpu.get_barrier_semaphore()
    peers = [at_z(k) for k in range(1, nz)] + [at_x(k) for k in range(1, nx)]
    peers += [(lax.rem(dp + k, 2 * ny), seq) for k in range(1, 2 * ny)]
    for peer in peers:
        pl.semaphore_signal(barrier, inc=1, device_id=peer, device_id_type=MESH)

    loads = []
    for i, (src, dst) in enumerate(
        [(v_hbm, vin), (k_hbm, kin), (q_hbm, qin), (u_hbm, uin), (w_hbm, win)]
    ):
        source = src.at[0] if i < 4 else src
        loads.append(pltpu.make_async_copy(source, dst, load_sem.at[i]))
        loads[-1].start()

    seen = vis_ref[...].astype(F32)
    rows = sz.rows
    upto = (
        lax.broadcasted_iota(jnp.int32, (rows, rows), 0)
        <= lax.broadcasted_iota(jnp.int32, (rows, rows), 1)
    )
    count = nn(jnp.broadcast_to(seen, (16, rows)).astype(BF16), jnp.where(upto, 1.0, 0.0).astype(BF16))
    rank = count[0:1, :].astype(jnp.int32) - 1
    odd = lax.rem(z, 2)
    slot = jnp.where(odd == 1, cap - 1 - rank, rank)
    slot = jnp.where(seen > 0.5, slot, -1)
    pick = jnp.where(lax.broadcasted_iota(jnp.int32, (cap, rows), 0) == slot, 1.0, 0.0)
    live = jnp.sum(pick, axis=1, keepdims=True)
    pick = pick.astype(BF16)

    for i in range(3):
        loads[i].wait()
    pv, pk, pq = nn(pick, vin[...]), nn(pick, kin[...]), nn(pick, qin[...])
    for h in range(heads):
        cols = slice(HEAD_DIM * h, HEAD_DIM * (h + 1))
        send_a[h] = jnp.concatenate(
            [pv[:, cols], pk[:, cols], pq[:, cols], jnp.broadcast_to(live, (cap, 16))], axis=1
        ).astype(BF16)

    pl.semaphore_wait(barrier, len(peers))

    def all_z(src, dst, ss, rs, start):
        copies = [remote(src(z_peer(k)), dst, ss.at[k - 1], rs.at[k - 1], at_z(k)) for k in range(1, nz)]
        if start:
            for copy in copies:
                copy.start()
        return copies

    a_copies = all_z(lambda t: send_a.at[t], recv_a.at[z], a_s, a_r, True)

    loads[3].wait()
    upk[...] = nn(pick, uin[...]).astype(BF16)
    loads[4].wait()
    send_b[...] = jnp.zeros_like(send_b)
    for h in range(heads):
        part = nt(upk[...], win[HEAD_DIM * h : HEAD_DIM * (h + 1), :])
        send_b[h, :, 0:HEAD_DIM] = part.astype(BF16)
    b_copies = all_z(lambda t: send_b.at[t], recv_b.at[z], b_s, b_r, True)

    recv_a[z] = send_a[z]
    recv_b[z] = send_b[z]
    eye = identity(256)
    unpick = nt(identity(rows), pick).astype(BF16)

    for copy in a_copies:
        copy.wait()
    flag = jnp.where(lane_iota(1, 256) >= 240, 1.0, 0.0)
    base = pl.multiple_of(x * nq, 16)
    for p in range(sz.pairs):
        both = recv_a[2 * p].astype(F32) + recv_a[2 * p + 1].astype(F32) - flag
        kv[pl.ds(base + p * cap, cap), :] = both.astype(BF16)
    g_copies = [
        remote(kv.at[pl.ds(base, nq)], kv.at[pl.ds(base, nq)], g_s.at[k - 1], g_r.at[k - 1], at_x(k))
        for k in range(1, nx)
    ]
    for copy in g_copies:
        copy.start()
    own = pltpu.roll(kv[pl.ds(base, nq), :].astype(F32), 256 - HEAD_DIM, 1)
    lanes = lane_iota(nq, 256)
    own = jnp.where((lanes >= HEAD_DIM) & (lanes < 2 * HEAD_DIM), own, 0.0)
    q_zero[...] = own.astype(BF16)
    q_mask[...] = jnp.where(lanes == 240, FAR, own).astype(BF16)

    def score_group(at):
        part = kv[pl.ds(at, nq), :]
        scores[pl.ds(at, nq), :] = nt(part, q_mask[...])

    score_group(base)

    for copy in b_copies:
        copy.wait()
    d_out[...] = jnp.zeros_like(d_out)
    for p in range(sz.pairs):
        both = recv_b[2 * p].astype(F32) + recv_b[2 * p + 1].astype(F32)
        d_out[p * cap : (p + 1) * cap, 0:128] = both.astype(BF16)
    d_out_t = nt(eye[0:HEAD_DIM, 0:128], d_out[:, 0:128])

    for k in range(1, nx):
        g_copies[k - 1].wait()
        score_group(pl.multiple_of(lax.rem(x + nx - k, nx) * nq, 16))

    steps = nk // blk

    def at_step(i):
        return pl.ds(pl.multiple_of(i * blk, blk), blk)

    def max_step(i, top):
        return jnp.maximum(top, jnp.max(scores[at_step(i), :], axis=0, keepdims=True))

    top = lax.fori_loop(0, steps, max_step, jnp.full((1, nq), -3e38, F32))

    def exp_step(i, total):
        e = jnp.exp((scores[at_step(i), :] - top) * scale)
        scores[at_step(i), :] = e
        kvt[:, at_step(i)] = nt(eye, kv[at_step(i), :]).astype(BF16)
        return total + jnp.sum(e, axis=0, keepdims=True)

    total = lax.fori_loop(0, steps, exp_step, jnp.zeros((1, nq), F32))
    inverse = 1.0 / total

    def attend_step(i, acc):
        w = (scores[at_step(i), :] * inverse).astype(BF16)
        return acc + nn(kvt[0:HEAD_DIM, at_step(i)], w)

    attended_t = lax.fori_loop(0, steps, attend_step, jnp.zeros((HEAD_DIM, nq), F32)).astype(BF16)
    eye_q = identity(nq)
    send_e[...] = jnp.zeros_like(send_e)
    attended = nt(eye_q, attended_t).astype(BF16)
    for p in range(sz.pairs):
        send_e[p, :, 0:HEAD_DIM] = attended[p * cap : (p + 1) * cap, :]
    e_copies = all_z(lambda t: send_e.at[lax.div(t, 2)], recv_e.at[z], e_s, e_r, True)
    recv_e[z] = send_e[lax.div(z, 2)]

    delta = jnp.sum(d_out_t * attended_t.astype(F32), axis=0, keepdims=True)
    slope = inverse * scale

    def back_step(i, acc):
        e = scores[at_step(i), :]
        w = (e * inverse).astype(BF16)
        grad_prob = nt(kv[at_step(i), :], d_out[...])
        ds = (e * slope * (grad_prob - delta)).astype(BF16)
        dkv[at_step(i), :] = (nn(ds, q_zero[...]) + nn(w, d_out[...])).astype(BF16)
        return acc + nn(kvt[HEAD_DIM : 2 * HEAD_DIM, at_step(i)], ds)

    dq_t = lax.fori_loop(0, steps, back_step, jnp.zeros((HEAD_DIM, nq), F32)).astype(BF16)

    c_copies = [
        remote(
            dkv.at[pl.ds(pl.multiple_of(x_peer(k) * nq, 16), nq)],
            recv_c.at[k - 1], c_s.at[k - 1], c_r.at[k - 1], at_x(k),
        )
        for k in range(1, nx)
    ]
    for copy in c_copies:
        copy.start()

    for copy in e_copies:
        copy.wait()
    half = heads // 2

    def weight_term(h):
        att = nt(eye[0:128, 0:128], recv_e[h])[0:HEAD_DIM, :].astype(BF16)
        return nn(att, upk[...])

    def other_half(i, carry):
        wsend1[i] = weight_term((1 - core) * half + i).astype(BF16)
        return carry

    lax.fori_loop(0, half, other_half, 0)
    w1 = remote(wsend1, wrecv1, w1_s, w1_r, (y * 2 + 1 - core, seq))
    w1.start()

    def own_half(i, carry):
        wown[i] = weight_term(core * half + i)
        return carry

    lax.fori_loop(0, half, own_half, 0)

    dq = nt(eye_q, dq_t)
    dq = jnp.concatenate(
        [jnp.zeros((nq, 2 * HEAD_DIM), F32), dq, jnp.zeros((nq, 16), F32)], axis=1
    )

    w1.wait()

    def join_half(i, carry):
        wown[i] = wown[i] + wrecv1[i].astype(F32)
        wsend2[i] = wown[i].astype(BF16)
        return carry

    lax.fori_loop(0, half, join_half, 0)
    w2 = [
        remote(
            wsend2.at[lax.rem(y + k, ny)], wrecv2.at[k - 1], w2_s.at[k - 1], w2_r.at[k - 1], at_y(k)
        )
        for k in range(1, ny)
    ]
    for copy in w2:
        copy.start()

    for copy in c_copies:
        copy.wait()
    mine = dkv[pl.ds(base, nq), :].astype(F32) + dq
    for k in range(1, nx):
        mine = mine + recv_c[k - 1].astype(F32)
    mine = mine.astype(BF16)
    for p in range(sz.pairs):
        send_d[p] = mine[p * cap : (p + 1) * cap, :]
    d_copies = all_z(lambda t: send_d.at[lax.div(t, 2)], recv_d.at[z], d_s, d_r, True)
    recv_d[z] = send_d[lax.div(z, 2)]

    for copy in w2:
        copy.wait()
    red[...] = wown[y]
    for k in range(1, ny):
        red[...] = red[...] + wrecv2[k - 1].astype(F32)
    tiles[...] = jnp.zeros_like(tiles)
    for r in range(HEAD_DIM // 16):
        for c in range(sz.col_tiles):
            tiles[r * sz.col_tiles + c] = red[16 * r : 16 * r + 16, 128 * c : 128 * c + 128].astype(BF16)
    share = sz.share
    w3 = [
        remote(
            tiles.at[pl.ds(z_peer(k) * share, share)],
            wrecv3.at[k - 1], w3_s.at[k - 1], w3_r.at[k - 1], at_z(k),
        )
        for k in range(1, nz)
    ]
    for copy in w3:
        copy.start()

    for copy in d_copies:
        copy.wait()
    stores = []
    for t, dst in enumerate((gv_hbm, gk_hbm, gq_hbm)):
        at = t * HEAD_DIM
        merged = jnp.concatenate(
            [recv_d[h].astype(F32)[:, at : at + HEAD_DIM] for h in range(heads)], axis=1
        ).astype(BF16)
        stage[t] = nn(unpick, merged).astype(BF16)
        stores.append(pltpu.make_async_copy(stage.at[t], dst.at[0], store_sem.at[t]))
        stores[-1].start()

    for copy in w3:
        copy.wait()
    part = tiles[pl.ds(z * share, share)].astype(F32)
    for k in range(1, nz):
        part = part + wrecv3[k - 1].astype(F32)
    wsend4[...] = part
    w4 = [
        remote(wsend4, wrecv4.at[k - 1], w4_s.at[k - 1], w4_r.at[k - 1], at_x(k)) for k in range(1, nx)
    ]
    for copy in w4:
        copy.start()
    for copy in w4:
        copy.wait()
    for k in range(1, nx):
        part = part + wrecv4[k - 1]
    wsend5[...] = part
    w5 = all_z(lambda t: wsend5, wrecv5.at[z], w5_s, w5_r, True)
    wrecv5[z] = wsend5[...]
    for copy in w5:
        copy.wait()
    for r in range(HEAD_DIM // 16):
        for c in range(sz.col_tiles):
            t = r * sz.col_tiles + c
            full[16 * r : 16 * r + 16, 128 * c : 128 * c + 128] = wrecv5[t // share, t % share]

    out_rows, per_head = sz.out_rows, sz.per_head
    head = lax.div(seq, per_head)
    owner = dp == lax.rem(head, half) * 2 + lax.div(head, half)
    w6 = [
        remote(gw_ref, gw_ref, w6_s.at[k - 1], w6_r, (lax.rem(dp + k, 2 * ny), seq))
        for k in range(1, 2 * ny)
    ]

    @pl.when(owner)
    def _():
        for q in range(per_head):

            @pl.when(lax.rem(seq, per_head) == q)
            def _():
                gw_ref[...] = full[out_rows * q : out_rows * (q + 1), :]

        for copy in w6:
            copy.start()
        for copy in w6:
            copy.wait_send()

    @pl.when(jnp.logical_not(owner))
    def _():
        w6[0].wait_recv()

    for copy in stores:
        copy.wait()


def per_device(sz, queries, keys, values, upstream, out_weight, visible):
    nx, nz, ny, cap, heads = sz.nx, sz.nz, sz.ny, sz.cap, sz.heads
    nq, nk, hd, width, rows = sz.queries, sz.keys, sz.hd, sz.width, sz.rows
    half, share = heads // 2, sz.share
    hbm = pl.BlockSpec(memory_space=pl.ANY)
    vmem = pl.BlockSpec(memory_space=pltpu.VMEM)
    grad = jax.ShapeDtypeStruct((1, rows, hd), BF16)
    dma = pltpu.SemaphoreType.DMA
    buffers = [
        ((rows, hd), BF16), ((rows, hd), BF16), ((rows, hd), BF16), ((rows, width), BF16), ((hd, width), BF16),
        ((heads, cap, 256), BF16), ((heads, cap, 256), BF16),
        ((heads, cap, 128), BF16), ((heads, cap, 128), BF16),
        ((nk, 256), BF16), ((256, nk), BF16), ((nq, 256), BF16), ((nq, 256), BF16), ((nq, 256), BF16),
        ((nk, nq), F32),
        ((sz.pairs, cap, 128), BF16), ((heads, cap, 128), BF16),
        ((nk, 256), BF16), ((nx - 1, nq, 256), BF16),
        ((sz.pairs, cap, 256), BF16), ((heads, cap, 256), BF16),
        ((cap, width), BF16),
        ((half, HEAD_DIM, width), F32), ((half, HEAD_DIM, width), BF16), ((half, HEAD_DIM, width), BF16),
        ((half, HEAD_DIM, width), BF16), ((ny - 1, HEAD_DIM, width), BF16),
        ((HEAD_DIM, width), F32),
        ((share * nz, 16, 128), BF16), ((nz - 1, share, 16, 128), BF16),
        ((share, 16, 128), F32), ((nx - 1, share, 16, 128), F32),
        ((share, 16, 128), F32), ((nz, share, 16, 128), F32),
        ((HEAD_DIM, width), F32), ((3, rows, hd), BF16),
    ]
    zs, xs, ys, one = dma((nz - 1,)), dma((nx - 1,)), dma((ny - 1,)), dma
    scratch = [pltpu.VMEM(shape, kind) for shape, kind in buffers]
    scratch += [dma((5,)), dma((3,))]
    scratch += [zs, zs, zs, zs, xs, xs, zs, zs, xs, xs, zs, zs]
    scratch += [one, one, ys, ys, zs, zs, xs, xs, zs, zs, dma((2 * ny - 1,)), one]
    return pl.pallas_call(
        functools.partial(kernel, sz),
        out_shape=(grad, grad, grad, jax.ShapeDtypeStruct((sz.out_rows, width), F32)),
        in_specs=[vmem] + [hbm] * 5,
        out_specs=(hbm, hbm, hbm, vmem),
        scratch_shapes=scratch,
        compiler_params=pltpu.CompilerParams(
            collective_id=0, has_side_effects=True, vmem_limit_bytes=56 * 1024 * 1024
        ),
    )(visible, queries, keys, values, upstream, out_weight)


def build(mesh, nz, ny, cap):
    n_seq = mesh.shape["seq"]

    def run(queries, keys, values, upstream, out_weight, visible):
        hd, width = out_weight.shape
        sz = Sizes(n_seq // nz, nz, ny, queries.shape[1], cap, hd // HEAD_DIM, width)
        return per_device(sz, queries, keys, values, upstream, out_weight, visible)

    part = P("dp", "seq", None)
    return jax.shard_map(
        run,
        mesh=mesh,
        in_specs=(part, part, part, part, P(), P("dp", "seq")),
        out_specs=(part, part, part, P("seq", None)),
        check_vma=False,
    )


def solution(mesh):
    return build(mesh, Z_RING, Y_RING, VIS_MAX)
```

```python
import functools

import jax
import jax.numpy as jnp
from jax import lax
from jax.experimental import pallas as pl
from jax.experimental.pallas import tpu as pltpu
from jax.sharding import PartitionSpec as P

HEAD_DIM = 80
VIS_MAX = 144
Z_RING = 8
Y_RING = 4

BF16 = jnp.bfloat16
F32 = jnp.float32
MESH = pl.DeviceIdType.MESH
FAR = 1e30


def nn(a, b):
    return jnp.dot(a, b, preferred_element_type=F32)


def nt(a, b):
    return lax.dot_general(a, b, (((1,), (1,)), ((), ())), preferred_element_type=F32)


def identity(n):
    rows = lax.broadcasted_iota(jnp.int32, (n, n), 0)
    cols = lax.broadcasted_iota(jnp.int32, (n, n), 1)
    return jnp.where(rows == cols, 1.0, 0.0).astype(BF16)


def lane_iota(rows, lanes):
    return lax.broadcasted_iota(jnp.int32, (rows, lanes), 1)


class Sizes:
    def __init__(self, nx, nz, ny, rows, cap, heads, width):
        self.nx, self.nz, self.ny = nx, nz, ny
        self.rows, self.cap, self.heads, self.width = rows, cap, heads, width
        self.pairs = nz // 2
        self.queries = self.pairs * cap
        self.keys = nx * self.queries
        self.hd = heads * HEAD_DIM
        self.half = width // 2
        self.col_tiles = self.half // 128
        self.tiles = (HEAD_DIM // 16) * self.col_tiles
        self.share = -(-self.tiles // self.pairs)
        self.out_rows = self.hd // (nx * nz)
        self.per_head = HEAD_DIM // self.out_rows


def kernel(
    sz,
    vis_ref, q_hbm, k_hbm, v_hbm, u_hbm, w_hbm,
    gq_hbm, gk_hbm, gv_hbm, gw_ref,
    qin, kin, vin, uin, win,
    send_a, recv_a, send_b, recv_b,
    kv, kvt, q_mask, q_zero, d_out, scores,
    send_e, recv_e, dkv, recv_c, send_d, recv_d,
    upk, upair, wown, wsend1, wrecv1, wsend2, wrecv2, red, tiles, wrecv3, wsend4, wrecv4, wsend5, wrecv5,
    full, stage,
    load_sem, store_sem, u_s, u_r,
    a_s, a_r, b_s, b_r, g_s, g_r, e_s, e_r, c_s, c_r, d_s, d_r,
    w1_s, w1_r, w2_s, w2_r, w3_s, w3_r, w4_s, w4_r, w5_s, w5_r, w6_s, w6_r,
):
    nx, nz, ny, cap, heads = sz.nx, sz.nz, sz.ny, sz.cap, sz.heads
    nq, half = sz.queries, sz.half
    scale = HEAD_DIM ** -0.5
    dp = lax.axis_index("dp")
    seq = lax.axis_index("seq")
    x, z = lax.div(seq, nz), lax.rem(seq, nz)
    y, core = lax.div(dp, 2), lax.rem(dp, 2)

    def z_peer(k):
        return lax.rem(z + k, nz)

    def x_peer(k):
        return lax.rem(x + k, nx)

    def at_z(k):
        return (dp, x * nz + z_peer(k))

    def at_x(k):
        return (dp, x_peer(k) * nz + z)

    def at_y(k):
        return (lax.rem(y + k, ny) * 2 + core, seq)

    def remote(src, dst, ss, rs, dev):
        return pltpu.make_async_remote_copy(
            src_ref=src, dst_ref=dst, send_sem=ss, recv_sem=rs, device_id=dev, device_id_type=MESH
        )

    barrier = pltpu.get_barrier_semaphore()
    peers = [at_z(k) for k in range(1, nz)] + [at_x(k) for k in range(1, nx)]
    peers += [(lax.rem(dp + k, 2 * ny), seq) for k in range(1, 2 * ny)]
    for peer in peers:
        pl.semaphore_signal(barrier, inc=1, device_id=peer, device_id_type=MESH)

    loads = []
    for i, (src, dst) in enumerate(
        [(v_hbm, vin), (k_hbm, kin), (q_hbm, qin), (u_hbm, uin), (w_hbm, win)]
    ):
        source = src.at[0] if i < 4 else src
        loads.append(pltpu.make_async_copy(source, dst, load_sem.at[i]))
        loads[-1].start()

    seen = vis_ref[...].astype(F32)
    rows = sz.rows
    upto = (
        lax.broadcasted_iota(jnp.int32, (rows, rows), 0)
        <= lax.broadcasted_iota(jnp.int32, (rows, rows), 1)
    )
    count = nn(jnp.broadcast_to(seen, (16, rows)).astype(BF16), jnp.where(upto, 1.0, 0.0).astype(BF16))
    rank = count[0:1, :].astype(jnp.int32) - 1
    odd = lax.rem(z, 2)
    slot = jnp.where(odd == 1, cap - 1 - rank, rank)
    slot = jnp.where(seen > 0.5, slot, -1)
    pick = jnp.where(lax.broadcasted_iota(jnp.int32, (cap, rows), 0) == slot, 1.0, 0.0)
    live = jnp.sum(pick, axis=1, keepdims=True)
    pick = pick.astype(BF16)

    for i in range(3):
        loads[i].wait()
    pv, pk, pq = nn(pick, vin[...]), nn(pick, kin[...]), nn(pick, qin[...])
    for h in range(heads):
        cols = slice(HEAD_DIM * h, HEAD_DIM * (h + 1))
        send_a[h] = jnp.concatenate(
            [pv[:, cols], pk[:, cols], pq[:, cols], jnp.broadcast_to(live, (cap, 16))], axis=1
        ).astype(BF16)

    pl.semaphore_wait(barrier, len(peers))

    def all_z(src, dst, ss, rs, start):
        copies = [remote(src(z_peer(k)), dst, ss.at[k - 1], rs.at[k - 1], at_z(k)) for k in range(1, nz)]
        if start:
            for copy in copies:
                copy.start()
        return copies

    a_copies = all_z(lambda t: send_a.at[t], recv_a.at[z], a_s, a_r, True)

    loads[3].wait()
    upk[...] = nn(pick, uin[...]).astype(BF16)
    loads[4].wait()
    send_b[...] = jnp.zeros_like(send_b)
    for h in range(heads):
        part = nt(upk[...], win[HEAD_DIM * h : HEAD_DIM * (h + 1), :])
        send_b[h, :, 0:HEAD_DIM] = part.astype(BF16)

    recv_a[z] = send_a[z]
    recv_b[z] = send_b[z]
    eye = identity(256)
    unpick = nt(identity(rows), pick).astype(BF16)

    for copy in a_copies:
        copy.wait()
    flag = jnp.where(lane_iota(1, 256) >= 240, 1.0, 0.0)
    base = pl.multiple_of(x * nq, 16)
    for p in range(sz.pairs):
        both = recv_a[2 * p].astype(F32) + recv_a[2 * p + 1].astype(F32) - flag
        kv[pl.ds(base + p * cap, cap), :] = both.astype(BF16)
    g_copies = [
        remote(kv.at[pl.ds(base, nq)], kv.at[pl.ds(base, nq)], g_s.at[k - 1], g_r.at[k - 1], at_x(k))
        for k in range(1, nx)
    ]
    for copy in g_copies:
        copy.start()
    b_copies = all_z(lambda t: send_b.at[t], recv_b.at[z], b_s, b_r, True)
    u_copy = remote(upk, upair, u_s, u_r, (dp, x * nz + lax.div(z, 2) * 2 + 1 - odd))
    u_copy.start()
    own = pltpu.roll(kv[pl.ds(base, nq), :].astype(F32), 256 - HEAD_DIM, 1)
    lanes = lane_iota(nq, 256)
    own = jnp.where((lanes >= HEAD_DIM) & (lanes < 2 * HEAD_DIM), own, 0.0)
    q_zero[...] = own.astype(BF16)
    q_mask[...] = jnp.where(lanes == 240, FAR, own).astype(BF16)

    def group(k):
        g = lax.rem(x + nx - k, nx)
        return g, pl.ds(pl.multiple_of(g * nq, 16), nq)

    def score_group(k, top):
        g, at = group(k)
        part = kv[at, :]
        value = nt(part, q_mask[...])
        scores[at, :] = value
        kvt[g] = nt(eye, part).astype(BF16)
        return jnp.maximum(top, jnp.max(value, axis=0, keepdims=True))

    top = score_group(0, jnp.full((1, nq), -3e38, F32))

    for copy in b_copies:
        copy.wait()
    d_out[...] = jnp.zeros_like(d_out)
    for p in range(sz.pairs):
        both = recv_b[2 * p].astype(F32) + recv_b[2 * p + 1].astype(F32)
        d_out[p * cap : (p + 1) * cap, 0:128] = both.astype(BF16)
    d_out_t = nt(eye[0:HEAD_DIM, 0:128], d_out[:, 0:128])

    for k in range(1, nx):
        g_copies[k - 1].wait()
        top = score_group(k, top)

    total = jnp.zeros((1, nq), F32)
    for k in range(nx):
        _, at = group(k)
        e = jnp.exp((scores[at, :] - top) * scale)
        scores[at, :] = e
        total = total + jnp.sum(e, axis=0, keepdims=True)
    inverse = 1.0 / total

    attended_t = jnp.zeros((HEAD_DIM, nq), F32)
    for k in range(nx):
        g, at = group(k)
        w = (scores[at, :] * inverse).astype(BF16)
        attended_t = attended_t + nn(kvt[g, 0:HEAD_DIM, :], w)
    attended_t = attended_t.astype(BF16)
    eye_q = identity(nq)
    send_e[...] = jnp.zeros_like(send_e)
    attended = nt(eye_q, attended_t).astype(BF16)
    for p in range(sz.pairs):
        send_e[p, :, 0:HEAD_DIM] = attended[p * cap : (p + 1) * cap, :]

    side = lax.div(z, ny)
    e_copies = []
    for p in range(sz.pairs):
        target = 2 * p + side
        copy = remote(
            send_e.at[p], recv_e.at[lax.rem(z, ny)], e_s.at[p], e_r.at[lax.rem(z, ny)], (dp, x * nz + target)
        )
        e_copies.append((copy, target != z))

        @pl.when(target != z)
        def _():
            copy.start()

        @pl.when(target == z)
        def _():
            recv_e[lax.rem(z, ny)] = send_e[p]

    delta = jnp.sum(d_out_t * attended_t.astype(F32), axis=0, keepdims=True)
    slope = inverse * scale

    dq_t = jnp.zeros((HEAD_DIM, nq), F32)
    c_copies = []
    for k in list(range(1, nx)) + [0]:
        g, at = group(k)
        e = scores[at, :]
        w = (e * inverse).astype(BF16)
        grad_prob = nt(kv[at, :], d_out[...])
        ds = (e * slope * (grad_prob - delta)).astype(BF16)
        dkv[at, :] = (nn(ds, q_zero[...]) + nn(w, d_out[...])).astype(BF16)
        if k:
            copy = remote(
                dkv.at[at], recv_c.at[k - 1], c_s.at[k - 1], c_r.at[k - 1], (dp, g * nz + z)
            )
            copy.start()
            c_copies.append(copy)
        dq_t = dq_t + nn(kvt[g, HEAD_DIM : 2 * HEAD_DIM, :], ds)
    dq_t = dq_t.astype(BF16)

    u_copy.wait()
    upk_all = (upk[...].astype(F32) + upair[...].astype(F32)).astype(BF16)
    upair[...] = upk_all
    for i in range(ny):
        source = odd * ny + i

        @pl.when(source != z)
        def _():
            remote(send_e.at[0], recv_e.at[i], e_s.at[0], e_r.at[i], (dp, x * nz + source)).wait_recv()

    for copy, away in e_copies:

        @pl.when(away)
        def _():
            copy.wait_send()

    terms = [nt(eye[0:128, 0:128], recv_e[i])[0:HEAD_DIM, :].astype(BF16) for i in range(ny)]
    other_cols = pl.ds(pl.multiple_of((1 - core) * half, 128), half)
    own_cols = pl.ds(pl.multiple_of(core * half, 128), half)
    for i in range(ny):
        wsend1[i] = nn(terms[i], upair[:, other_cols]).astype(BF16)
    w1 = remote(wsend1, wrecv1, w1_s, w1_r, (y * 2 + 1 - core, seq))
    w1.start()
    for i in range(ny):
        wown[i] = nn(terms[i], upair[:, own_cols])

    dq = nt(eye_q, dq_t)
    dq = jnp.concatenate(
        [jnp.zeros((nq, 2 * HEAD_DIM), F32), dq, jnp.zeros((nq, 16), F32)], axis=1
    )

    w1.wait()

    for i in range(ny):
        wown[i] = wown[i] + wrecv1[i].astype(F32)
        wsend2[i] = wown[i].astype(BF16)
    w2 = [
        remote(
            wsend2.at[lax.rem(y + k, ny)], wrecv2.at[k - 1], w2_s.at[k - 1], w2_r.at[k - 1], at_y(k)
        )
        for k in range(1, ny)
    ]
    for copy in w2:
        copy.start()

    for copy in c_copies:
        copy.wait()
    mine = dkv[pl.ds(base, nq), :].astype(F32) + dq
    for k in range(1, nx):
        mine = mine + recv_c[k - 1].astype(F32)
    mine = mine.astype(BF16)
    for p in range(sz.pairs):
        send_d[p] = mine[p * cap : (p + 1) * cap, :]
    d_copies = all_z(lambda t: send_d.at[lax.div(t, 2)], recv_d.at[z], d_s, d_r, True)
    recv_d[z] = send_d[lax.div(z, 2)]

    for copy in w2:
        copy.wait()
    red[...] = wown[y]
    for k in range(1, ny):
        red[...] = red[...] + wrecv2[k - 1].astype(F32)
    tiles[...] = jnp.zeros_like(tiles)
    for r in range(HEAD_DIM // 16):
        for c in range(sz.col_tiles):
            tiles[r * sz.col_tiles + c] = red[16 * r : 16 * r + 16, 128 * c : 128 * c + 128].astype(BF16)
    share = sz.share
    w3 = [
        remote(
            tiles.at[pl.ds(lax.div(z_peer(2 * k), 2) * share, share)],
            wrecv3.at[k - 1], w3_s.at[k - 1], w3_r.at[k - 1], at_z(2 * k),
        )
        for k in range(1, sz.pairs)
    ]
    for copy in w3:
        copy.start()

    for copy in d_copies:
        copy.wait()
    stores = []
    for t, dst in enumerate((gv_hbm, gk_hbm, gq_hbm)):
        at = t * HEAD_DIM
        merged = jnp.concatenate(
            [recv_d[h].astype(F32)[:, at : at + HEAD_DIM] for h in range(heads)], axis=1
        ).astype(BF16)
        stage[t] = nn(unpick, merged).astype(BF16)
        stores.append(pltpu.make_async_copy(stage.at[t], dst.at[0], store_sem.at[t]))
        stores[-1].start()

    for copy in w3:
        copy.wait()
    part = tiles[pl.ds(lax.div(z, 2) * share, share)].astype(F32)
    for k in range(1, sz.pairs):
        part = part + wrecv3[k - 1].astype(F32)
    wsend4[...] = part
    per_head, out_rows = sz.per_head, sz.out_rows
    head = odd * ny + y
    row = lax.div(head * per_head, nz)
    w4 = [
        remote(wsend4, wrecv4.at[k - 1], w4_s.at[k - 1], w4_r.at[k - 1], at_x(k)) for k in range(1, nx)
    ]
    for k in range(1, nx):

        @pl.when(x_peer(k) == row)
        def _():
            w4[k - 1].start()

    first = lax.rem(head * per_head, nz)
    w5 = [
        remote(
            wsend5, wrecv5.at[lax.div(z, 2)], w5_s.at[q], w5_r.at[lax.div(z, 2)], (dp, x * nz + first + q)
        )
        for q in range(per_head)
    ]

    @pl.when(x == row)
    def _():
        for copy in w4:
            copy.wait_recv()
        summed = wsend4[...]
        for k in range(1, nx):
            summed = summed + wrecv4[k - 1]
        wsend5[...] = summed.astype(BF16)
        for q in range(per_head):

            @pl.when(first + q != z)
            def _():
                w5[q].start()

            @pl.when(first + q == z)
            def _():
                wrecv5[lax.div(z, 2)] = wsend5[...]

    block = lax.div(seq, per_head)
    owner = y == lax.rem(block, ny)
    w6 = [
        remote(
            gw_ref.at[:, own_cols], gw_ref.at[:, own_cols], w6_s.at[k - 1], w6_r.at[core],
            (lax.rem(dp + k, 2 * ny), seq),
        )
        for k in range(1, 2 * ny)
    ]
    w6_other = remote(
        gw_ref.at[:, other_cols], gw_ref.at[:, other_cols], w6_s.at[0], w6_r.at[1 - core],
        (y * 2 + 1 - core, seq),
    )

    @pl.when(owner)
    def _():
        for j in range(sz.pairs):
            source = 2 * j + lax.div(block, ny)

            @pl.when(source != z)
            def _():
                remote(
                    wsend5, wrecv5.at[j], w5_s.at[0], w5_r.at[j], (dp, x * nz + source)
                ).wait_recv()

        for r in range(HEAD_DIM // 16):
            for c in range(sz.col_tiles):
                t = r * sz.col_tiles + c
                full[16 * r : 16 * r + 16, 128 * c : 128 * c + 128] = wrecv5[t // share, t % share].astype(F32)
        for q in range(per_head):

            @pl.when(lax.rem(seq, per_head) == q)
            def _():
                gw_ref[:, own_cols] = full[out_rows * q : out_rows * (q + 1), :]

        for copy in w6:
            copy.start()

    @pl.when(jnp.logical_not(owner))
    def _():
        w6[0].wait_recv()

    w6_other.wait_recv()

    @pl.when(owner)
    def _():
        for copy in w6:
            copy.wait_send()

    @pl.when(x == row)
    def _():
        for q in range(per_head):

            @pl.when(first + q != z)
            def _():
                w5[q].wait_send()

    for k in range(1, nx):

        @pl.when(x_peer(k) == row)
        def _():
            w4[k - 1].wait_send()

    for copy in stores:
        copy.wait()


def per_device(sz, queries, keys, values, upstream, out_weight, visible):
    nx, nz, ny, cap, heads = sz.nx, sz.nz, sz.ny, sz.cap, sz.heads
    nq, nk, hd, width, rows = sz.queries, sz.keys, sz.hd, sz.width, sz.rows
    half, share, pairs = sz.half, sz.share, sz.pairs
    hbm = pl.BlockSpec(memory_space=pl.ANY)
    vmem = pl.BlockSpec(memory_space=pltpu.VMEM)
    grad = jax.ShapeDtypeStruct((1, rows, hd), BF16)
    dma = pltpu.SemaphoreType.DMA
    buffers = [
        ((rows, hd), BF16), ((rows, hd), BF16), ((rows, hd), BF16), ((rows, width), BF16), ((hd, width), BF16),
        ((heads, cap, 256), BF16), ((heads, cap, 256), BF16),
        ((heads, cap, 128), BF16), ((heads, cap, 128), BF16),
        ((nk, 256), BF16), ((nx, 256, nq), BF16), ((nq, 256), BF16), ((nq, 256), BF16), ((nq, 256), BF16),
        ((nk, nq), F32),
        ((pairs, cap, 128), BF16), ((ny, cap, 128), BF16),
        ((nk, 256), BF16), ((nx - 1, nq, 256), BF16),
        ((sz.pairs, cap, 256), BF16), ((heads, cap, 256), BF16),
        ((cap, width), BF16), ((cap, width), BF16),
        ((ny, HEAD_DIM, half), F32), ((ny, HEAD_DIM, half), BF16), ((ny, HEAD_DIM, half), BF16),
        ((ny, HEAD_DIM, half), BF16), ((ny - 1, HEAD_DIM, half), BF16),
        ((HEAD_DIM, half), F32),
        ((share * pairs, 16, 128), BF16), ((pairs - 1, share, 16, 128), BF16),
        ((share, 16, 128), F32), ((nx - 1, share, 16, 128), F32),
        ((share, 16, 128), BF16), ((pairs, share, 16, 128), BF16),
        ((HEAD_DIM, half), F32), ((3, rows, hd), BF16),
    ]
    zs, xs, ys, ps, one = dma((nz - 1,)), dma((nx - 1,)), dma((ny - 1,)), dma((pairs,)), dma
    scratch = [pltpu.VMEM(shape, kind) for shape, kind in buffers]
    scratch += [dma((5,)), dma((3,)), one, one]
    scratch += [zs, zs, zs, zs, xs, xs, ps, dma((ny,)), xs, xs, zs, zs]
    scratch += [one, one, ys, ys, dma((pairs - 1,)), dma((pairs - 1,)), xs, xs]
    scratch += [dma((sz.per_head,)), ps, dma((2 * ny - 1,)), dma((2,))]
    return pl.pallas_call(
        functools.partial(kernel, sz),
        out_shape=(grad, grad, grad, jax.ShapeDtypeStruct((sz.out_rows, width), F32)),
        in_specs=[vmem] + [hbm] * 5,
        out_specs=(hbm, hbm, hbm, vmem),
        scratch_shapes=scratch,
        compiler_params=pltpu.CompilerParams(
            collective_id=0, has_side_effects=True, vmem_limit_bytes=56 * 1024 * 1024
        ),
    )(visible, queries, keys, values, upstream, out_weight)


def build(mesh, nz, ny, cap):
    n_seq = mesh.shape["seq"]

    def run(queries, keys, values, upstream, out_weight, visible):
        hd, width = out_weight.shape
        sz = Sizes(n_seq // nz, nz, ny, queries.shape[1], cap, hd // HEAD_DIM, width)
        return per_device(sz, queries, keys, values, upstream, out_weight, visible)

    part = P("dp", "seq", None)
    return jax.shard_map(
        run,
        mesh=mesh,
        in_specs=(part, part, part, part, P(), P("dp", "seq")),
        out_specs=(part, part, part, P("seq", None)),
        check_vma=False,
    )


def solution(mesh):
    return build(mesh, Z_RING, Y_RING, VIS_MAX)
```

```python
import functools

import jax
import jax.numpy as jnp
from jax import lax
from jax.experimental import pallas as pl
from jax.experimental.pallas import tpu as pltpu
from jax.sharding import PartitionSpec as P

HEAD_DIM = 80
VIS_MAX = 144
Z_RING = 8
Y_RING = 4

BF16 = jnp.bfloat16
F32 = jnp.float32
MESH = pl.DeviceIdType.MESH
FAR = 1e30
DEAD = 64.0


def nn(a, b):
    return jnp.dot(a, b, preferred_element_type=F32)


def nt(a, b):
    return lax.dot_general(a, b, (((1,), (1,)), ((), ())), preferred_element_type=F32)


def identity(n):
    rows = lax.broadcasted_iota(jnp.int32, (n, n), 0)
    cols = lax.broadcasted_iota(jnp.int32, (n, n), 1)
    return jnp.where(rows == cols, 1.0, 0.0).astype(BF16)


def fold(tail):
    third = tail.shape[0] // 3
    parts = [tail[j * third : (j + 1) * third, :] for j in range(3)]
    return jnp.concatenate(parts + [jnp.zeros((third, 8), F32)], axis=1)


def unfold(folded):
    return jnp.concatenate([folded[:, 40 * j : 40 * j + 40] for j in range(3)], axis=0)


def lane_iota(rows, lanes):
    return lax.broadcasted_iota(jnp.int32, (rows, lanes), 1)


class Sizes:
    def __init__(self, nx, nz, ny, rows, cap, heads, width):
        self.nx, self.nz, self.ny = nx, nz, ny
        self.rows, self.cap, self.heads, self.width = rows, cap, heads, width
        self.pairs = nz // 2
        self.queries = self.pairs * cap
        self.keys = nx * self.queries
        self.hd = heads * HEAD_DIM
        self.half = width // 2
        self.col_tiles = self.half // 128
        self.tiles = (HEAD_DIM // 16) * self.col_tiles
        self.share = -(-self.tiles // self.pairs)
        self.out_rows = self.hd // (nx * nz)
        self.per_head = HEAD_DIM // self.out_rows


def kernel(
    sz,
    vis_ref, q_hbm, k_hbm, v_hbm, u_hbm, w_hbm,
    gq_hbm, gk_hbm, gv_hbm, gw_ref,
    qin, kin, vin, uin, win,
    send_a, recv_a, send_b, recv_b,
    send_g, recv_g, kv, kvt, q_mask, q_zero, d_out, scores,
    send_e, recv_e, dkv, send_c, recv_c, send_f, recv_f, send_d, recv_d,
    upk, upair, wown, wsend1, wrecv1, wsend2, wrecv2, red, tiles, wrecv3, wsend4, wrecv4, wsend5, wrecv5,
    full, stage,
    load_sem, store_sem, u_s, u_r, f_s, f_r,
    a_s, a_r, b_s, b_r, g_s, g_r, e_s, e_r, c_s, c_r, d_s, d_r,
    w1_s, w1_r, w2_s, w2_r, w3_s, w3_r, w4_s, w4_r, w5_s, w5_r, w6_s, w6_r,
):
    nx, nz, ny, cap, heads = sz.nx, sz.nz, sz.ny, sz.cap, sz.heads
    nq, half = sz.queries, sz.half
    scale = HEAD_DIM ** -0.5
    dp = lax.axis_index("dp")
    seq = lax.axis_index("seq")
    x, z = lax.div(seq, nz), lax.rem(seq, nz)
    y, core = lax.div(dp, 2), lax.rem(dp, 2)

    def z_peer(k):
        return lax.rem(z + k, nz)

    def x_peer(k):
        return lax.rem(x + k, nx)

    def at_z(k):
        return (dp, x * nz + z_peer(k))

    def at_x(k):
        return (dp, x_peer(k) * nz + z)

    def at_y(k):
        return (lax.rem(y + k, ny) * 2 + core, seq)

    def remote(src, dst, ss, rs, dev):
        return pltpu.make_async_remote_copy(
            src_ref=src, dst_ref=dst, send_sem=ss, recv_sem=rs, device_id=dev, device_id_type=MESH
        )

    barrier = pltpu.get_barrier_semaphore()
    peers = [at_z(k) for k in range(1, nz)] + [at_x(k) for k in range(1, nx)]
    peers += [(lax.rem(dp + k, 2 * ny), seq) for k in range(1, 2 * ny)]
    for peer in peers:
        pl.semaphore_signal(barrier, inc=1, device_id=peer, device_id_type=MESH)

    loads = []
    for i, (src, dst) in enumerate(
        [(v_hbm, vin), (k_hbm, kin), (q_hbm, qin), (u_hbm, uin), (w_hbm, win)]
    ):
        source = src.at[0] if i < 4 else src
        loads.append(pltpu.make_async_copy(source, dst, load_sem.at[i]))
        loads[-1].start()

    seen = vis_ref[...].astype(F32)
    rows = sz.rows
    upto = (
        lax.broadcasted_iota(jnp.int32, (rows, rows), 0)
        <= lax.broadcasted_iota(jnp.int32, (rows, rows), 1)
    )
    count = nn(jnp.broadcast_to(seen, (16, rows)).astype(BF16), jnp.where(upto, 1.0, 0.0).astype(BF16))
    rank = count[0:1, :].astype(jnp.int32) - 1
    odd = lax.rem(z, 2)
    slot = jnp.where(odd == 1, cap - 1 - rank, rank)
    slot = jnp.where(seen > 0.5, slot, -1)
    pick = jnp.where(lax.broadcasted_iota(jnp.int32, (cap, rows), 0) == slot, 1.0, 0.0)
    live = jnp.sum(pick, axis=1, keepdims=True)
    pick = pick.astype(BF16)

    loads[0].wait()
    loads[1].wait()
    pv, pk = nn(pick, vin[...]), nn(pick, kin[...])
    flags = jnp.broadcast_to(live, (cap, 8))

    def put(dst, h, left, right, extra):
        dst[h, 0:cap, :] = jnp.concatenate([left, right[:, 0:48]], axis=1).astype(BF16)
        dst[h, cap:, :] = fold(jnp.concatenate([right[:, 48:80], extra], axis=1)).astype(BF16)

    def head_cols(h):
        return slice(HEAD_DIM * h, HEAD_DIM * (h + 1))

    for h in range(heads):
        put(send_a, h, pv[:, head_cols(h)], pk[:, head_cols(h)], flags)

    pl.semaphore_wait(barrier, len(peers))

    def all_z(src, dst, ss, rs, start):
        copies = [remote(src(z_peer(k)), dst, ss.at[k - 1], rs.at[k - 1], at_z(k)) for k in range(1, nz)]
        if start:
            for copy in copies:
                copy.start()
        return copies

    a_copies = all_z(lambda t: send_a.at[t], recv_a.at[z], a_s, a_r, True)

    loads[2].wait()
    pq = nn(pick, qin[...])
    loads[3].wait()
    upk[...] = nn(pick, uin[...]).astype(BF16)
    loads[4].wait()
    for h in range(heads):
        part = nt(upk[...], win[HEAD_DIM * h : HEAD_DIM * (h + 1), :])
        put(send_b, h, pq[:, head_cols(h)], part, jnp.zeros((cap, 8), F32))

    recv_a[z] = send_a[z]
    recv_b[z] = send_b[z]
    eye = identity(256)
    unpick = nt(identity(rows), pick).astype(BF16)

    for copy in a_copies:
        copy.wait()
    base = pl.multiple_of(x * nq, 16)
    tails = []
    for p in range(sz.pairs):
        both = recv_a[2 * p].astype(F32) + recv_a[2 * p + 1].astype(F32)
        main, rest = both[0:cap, :], unfold(both[cap:, :])
        dead = rest[:, 32:33] < 0.5
        tails.append(rest[:, 0:32])
        mask = jnp.broadcast_to(jnp.where(dead, -1.0, 0.0), (cap, 96))
        kv[pl.ds(base + p * cap, cap), :] = jnp.concatenate([main, rest[:, 0:32], mask], axis=1).astype(BF16)
        marked = jnp.where(dead & (lane_iota(cap, 128) == 0), DEAD, main)
        send_g[p * cap : (p + 1) * cap, :] = marked.astype(BF16)
    send_g[nq:, 0 : 32 * sz.pairs] = jnp.concatenate(tails, axis=1).astype(BF16)
    g_copies = [
        remote(send_g, recv_g.at[k - 1], g_s.at[k - 1], g_r.at[k - 1], at_x(k)) for k in range(1, nx)
    ]
    for copy in g_copies:
        copy.start()
    b_copies = all_z(lambda t: send_b.at[t], recv_b.at[z], b_s, b_r, True)
    u_copy = remote(upk, upair, u_s, u_r, (dp, x * nz + lax.div(z, 2) * 2 + 1 - odd))
    u_copy.start()
    for copy in b_copies:
        copy.wait()
    for p in range(sz.pairs):
        both = recv_b[2 * p].astype(F32) + recv_b[2 * p + 1].astype(F32)
        main, rest = both[0:cap, :], unfold(both[cap:, :])
        at = slice(p * cap, (p + 1) * cap)
        query = jnp.concatenate(
            [jnp.zeros((cap, 80), F32), main[:, 0:80], jnp.zeros((cap, 96), F32)], axis=1
        )
        q_zero[at, :] = query.astype(BF16)
        q_mask[at, :] = jnp.where(lane_iota(cap, 256) == 240, FAR, query).astype(BF16)
        d_out[at, :] = jnp.concatenate(
            [main[:, 80:128], rest[:, 0:32], jnp.zeros((cap, 176), F32)], axis=1
        ).astype(BF16)

    def group(k):
        g = lax.rem(x + nx - k, nx)
        return g, pl.ds(pl.multiple_of(g * nq, 16), nq)

    def score_group(k, top):
        g, at = group(k)
        part = kv[at, :]
        value = nt(part, q_mask[...])
        scores[at, :] = value
        kvt[g] = nt(eye, part).astype(BF16)
        return jnp.maximum(top, jnp.max(value, axis=0, keepdims=True))

    top = score_group(0, jnp.full((1, nq), -3e38, F32))

    d_out_t = nt(eye[0:HEAD_DIM, 0:128], d_out[:, 0:128])

    for k in range(1, nx):
        g_copies[k - 1].wait()
        _, at = group(k)
        for p in range(sz.pairs):
            main = recv_g[k - 1, p * cap : (p + 1) * cap, :].astype(F32)
            rest = recv_g[k - 1, nq:, :].astype(F32)[:, 32 * p : 32 * p + 32]
            mask = jnp.broadcast_to(jnp.where(main[:, 0:1] > DEAD / 2, -1.0, 0.0), (cap, 96))
            start = pl.multiple_of(at.start + p * cap, 16)
            kv[pl.ds(start, cap), :] = jnp.concatenate([main, rest, mask], axis=1).astype(BF16)
        top = score_group(k, top)

    total = jnp.zeros((1, nq), F32)
    for k in range(nx):
        _, at = group(k)
        e = jnp.exp((scores[at, :] - top) * scale)
        scores[at, :] = e
        total = total + jnp.sum(e, axis=0, keepdims=True)
    inverse = 1.0 / total

    attended_t = jnp.zeros((HEAD_DIM, nq), F32)
    for k in range(nx):
        g, at = group(k)
        w = (scores[at, :] * inverse).astype(BF16)
        attended_t = attended_t + nn(kvt[g, 0:HEAD_DIM, :], w)
    attended_t = attended_t.astype(BF16)
    eye_q = identity(nq)
    send_e[...] = jnp.zeros_like(send_e)
    attended = nt(eye_q, attended_t).astype(BF16)
    for p in range(sz.pairs):
        send_e[p, :, 0:HEAD_DIM] = attended[p * cap : (p + 1) * cap, :]

    side = lax.div(z, ny)
    e_copies = []
    for p in range(sz.pairs):
        target = 2 * p + side
        copy = remote(
            send_e.at[p], recv_e.at[lax.rem(z, ny)], e_s.at[p], e_r.at[lax.rem(z, ny)], (dp, x * nz + target)
        )
        e_copies.append((copy, target != z))

        @pl.when(target != z)
        def _():
            copy.start()

        @pl.when(target == z)
        def _():
            recv_e[lax.rem(z, ny)] = send_e[p]

    delta = jnp.sum(d_out_t * attended_t.astype(F32), axis=0, keepdims=True)
    slope = inverse * scale

    dq_t = jnp.zeros((HEAD_DIM, nq), F32)
    c_copies = []
    for k in list(range(1, nx)) + [0]:
        g, at = group(k)
        e = scores[at, :]
        w = (e * inverse).astype(BF16)
        grad_prob = nt(kv[at, :], d_out[...])
        ds = (e * slope * (grad_prob - delta)).astype(BF16)
        term = nn(ds, q_zero[...]) + nn(w, d_out[...])
        if k == 0:
            dkv[...] = term
        else:
            send_c[k - 1, 0:nq, :] = term[:, 0:128].astype(BF16)
            send_c[k - 1, nq:, 0 : 32 * sz.pairs] = jnp.concatenate(
                [term[p * cap : (p + 1) * cap, 128:160] for p in range(sz.pairs)], axis=1
            ).astype(BF16)
            copy = remote(
                send_c.at[k - 1], recv_c.at[k - 1], c_s.at[k - 1], c_r.at[k - 1], (dp, g * nz + z)
            )
            copy.start()
            c_copies.append(copy)
        dq_t = dq_t + nn(kvt[g, HEAD_DIM : 2 * HEAD_DIM, :], ds)
    dq = nt(eye_q, dq_t.astype(BF16)).astype(BF16)
    send_f[...] = jnp.zeros_like(send_f)
    for p in range(sz.pairs):
        send_f[p, :, 0:HEAD_DIM] = dq[p * cap : (p + 1) * cap, :]
    f_copies = all_z(lambda t: send_f.at[lax.div(t, 2)], recv_f.at[z], f_s, f_r, True)
    recv_f[z] = send_f[lax.div(z, 2)]

    u_copy.wait()
    upk_all = (upk[...].astype(F32) + upair[...].astype(F32)).astype(BF16)
    upair[...] = upk_all
    for i in range(ny):
        source = odd * ny + i

        @pl.when(source != z)
        def _():
            remote(send_e.at[0], recv_e.at[i], e_s.at[0], e_r.at[i], (dp, x * nz + source)).wait_recv()

    for copy, away in e_copies:

        @pl.when(away)
        def _():
            copy.wait_send()

    terms = [nt(eye[0:128, 0:128], recv_e[i])[0:HEAD_DIM, :].astype(BF16) for i in range(ny)]
    other_cols = pl.ds(pl.multiple_of((1 - core) * half, 128), half)
    own_cols = pl.ds(pl.multiple_of(core * half, 128), half)
    for i in range(ny):
        wsend1[i] = nn(terms[i], upair[:, other_cols]).astype(BF16)
    w1 = remote(wsend1, wrecv1, w1_s, w1_r, (y * 2 + 1 - core, seq))
    w1.start()
    for i in range(ny):
        wown[i] = nn(terms[i], upair[:, own_cols])

    w1.wait()

    for i in range(ny):
        wown[i] = wown[i] + wrecv1[i].astype(F32)
        wsend2[i] = wown[i].astype(BF16)
    w2 = [
        remote(
            wsend2.at[lax.rem(y + k, ny)], wrecv2.at[k - 1], w2_s.at[k - 1], w2_r.at[k - 1], at_y(k)
        )
        for k in range(1, ny)
    ]
    for copy in w2:
        copy.start()

    for copy in c_copies:
        copy.wait()
    mine, rest = dkv[:, 0:128], jnp.zeros((cap, 128), F32)
    for k in range(1, nx):
        mine = mine + recv_c[k - 1, 0:nq, :].astype(F32)
        rest = rest + recv_c[k - 1, nq:, :].astype(F32)
    for p in range(sz.pairs):
        at = slice(p * cap, (p + 1) * cap)
        tail = dkv[at, 128:160] + rest[:, 32 * p : 32 * p + 32]
        send_d[p, 0:cap, :] = mine[at, :].astype(BF16)
        send_d[p, cap:, :] = fold(jnp.concatenate([tail, jnp.zeros((cap, 8), F32)], axis=1)).astype(BF16)
    d_copies = all_z(lambda t: send_d.at[lax.div(t, 2)], recv_d.at[z], d_s, d_r, True)
    recv_d[z] = send_d[lax.div(z, 2)]

    for copy in w2:
        copy.wait()
    red[...] = wown[y]
    for k in range(1, ny):
        red[...] = red[...] + wrecv2[k - 1].astype(F32)
    tiles[...] = jnp.zeros_like(tiles)
    for r in range(HEAD_DIM // 16):
        for c in range(sz.col_tiles):
            tiles[r * sz.col_tiles + c] = red[16 * r : 16 * r + 16, 128 * c : 128 * c + 128].astype(BF16)
    share = sz.share
    w3 = [
        remote(
            tiles.at[pl.ds(lax.div(z_peer(2 * k), 2) * share, share)],
            wrecv3.at[k - 1], w3_s.at[k - 1], w3_r.at[k - 1], at_z(2 * k),
        )
        for k in range(1, sz.pairs)
    ]
    for copy in w3:
        copy.start()

    stores = []

    def give(t, dst, parts):
        merged = jnp.concatenate(parts, axis=1).astype(BF16)
        stage[t] = nn(unpick, merged).astype(BF16)
        stores.append(pltpu.make_async_copy(stage.at[t], dst.at[0], store_sem.at[t]))
        stores[-1].start()

    for copy in f_copies:
        copy.wait()
    give(0, gq_hbm, [recv_f[h].astype(F32)[:, 0:HEAD_DIM] for h in range(heads)])
    for copy in d_copies:
        copy.wait()
    mains = [recv_d[h, 0:cap, :].astype(F32) for h in range(heads)]
    rests = [unfold(recv_d[h, cap:, :].astype(F32))[:, 0:32] for h in range(heads)]
    give(1, gv_hbm, [m[:, 0:HEAD_DIM] for m in mains])
    give(2, gk_hbm, [m for h in range(heads) for m in (mains[h][:, HEAD_DIM:], rests[h])])

    for copy in w3:
        copy.wait()
    part = tiles[pl.ds(lax.div(z, 2) * share, share)].astype(F32)
    for k in range(1, sz.pairs):
        part = part + wrecv3[k - 1].astype(F32)
    wsend4[...] = part
    per_head, out_rows = sz.per_head, sz.out_rows
    head = odd * ny + y
    row = lax.div(head * per_head, nz)
    w4 = [
        remote(wsend4, wrecv4.at[k - 1], w4_s.at[k - 1], w4_r.at[k - 1], at_x(k)) for k in range(1, nx)
    ]
    for k in range(1, nx):

        @pl.when(x_peer(k) == row)
        def _():
            w4[k - 1].start()

    first = lax.rem(head * per_head, nz)
    w5 = [
        remote(
            wsend5, wrecv5.at[lax.div(z, 2)], w5_s.at[q], w5_r.at[lax.div(z, 2)], (dp, x * nz + first + q)
        )
        for q in range(per_head)
    ]

    @pl.when(x == row)
    def _():
        for copy in w4:
            copy.wait_recv()
        summed = wsend4[...]
        for k in range(1, nx):
            summed = summed + wrecv4[k - 1]
        wsend5[...] = summed.astype(BF16)
        for q in range(per_head):

            @pl.when(first + q != z)
            def _():
                w5[q].start()

            @pl.when(first + q == z)
            def _():
                wrecv5[lax.div(z, 2)] = wsend5[...]

    block = lax.div(seq, per_head)
    owner = y == lax.rem(block, ny)
    w6 = [
        remote(
            gw_ref.at[:, own_cols], gw_ref.at[:, own_cols], w6_s.at[k - 1], w6_r.at[core],
            (lax.rem(dp + k, 2 * ny), seq),
        )
        for k in range(1, 2 * ny)
    ]
    w6_other = remote(
        gw_ref.at[:, other_cols], gw_ref.at[:, other_cols], w6_s.at[0], w6_r.at[1 - core],
        (y * 2 + 1 - core, seq),
    )

    @pl.when(owner)
    def _():
        for j in range(sz.pairs):
            source = 2 * j + lax.div(block, ny)

            @pl.when(source != z)
            def _():
                remote(
                    wsend5, wrecv5.at[j], w5_s.at[0], w5_r.at[j], (dp, x * nz + source)
                ).wait_recv()

        for r in range(HEAD_DIM // 16):
            for c in range(sz.col_tiles):
                t = r * sz.col_tiles + c
                full[16 * r : 16 * r + 16, 128 * c : 128 * c + 128] = wrecv5[t // share, t % share].astype(F32)
        for q in range(per_head):

            @pl.when(lax.rem(seq, per_head) == q)
            def _():
                gw_ref[:, own_cols] = full[out_rows * q : out_rows * (q + 1), :]

        for copy in w6:
            copy.start()

    @pl.when(jnp.logical_not(owner))
    def _():
        w6[0].wait_recv()

    w6_other.wait_recv()

    @pl.when(owner)
    def _():
        for copy in w6:
            copy.wait_send()

    @pl.when(x == row)
    def _():
        for q in range(per_head):

            @pl.when(first + q != z)
            def _():
                w5[q].wait_send()

    for k in range(1, nx):

        @pl.when(x_peer(k) == row)
        def _():
            w4[k - 1].wait_send()

    for copy in stores:
        copy.wait()


def per_device(sz, queries, keys, values, upstream, out_weight, visible):
    nx, nz, ny, cap, heads = sz.nx, sz.nz, sz.ny, sz.cap, sz.heads
    nq, nk, hd, width, rows = sz.queries, sz.keys, sz.hd, sz.width, sz.rows
    half, share, pairs = sz.half, sz.share, sz.pairs
    long, wide = cap + cap // 3, nq + cap
    hbm = pl.BlockSpec(memory_space=pl.ANY)
    vmem = pl.BlockSpec(memory_space=pltpu.VMEM)
    grad = jax.ShapeDtypeStruct((1, rows, hd), BF16)
    dma = pltpu.SemaphoreType.DMA
    buffers = [
        ((rows, hd), BF16), ((rows, hd), BF16), ((rows, hd), BF16), ((rows, width), BF16), ((hd, width), BF16),
        ((heads, long, 128), BF16), ((heads, long, 128), BF16),
        ((heads, long, 128), BF16), ((heads, long, 128), BF16),
        ((wide, 128), BF16), ((nx - 1, wide, 128), BF16),
        ((nk, 256), BF16), ((nx, 256, nq), BF16), ((nq, 256), BF16), ((nq, 256), BF16), ((nq, 256), BF16),
        ((nk, nq), F32),
        ((pairs, cap, 128), BF16), ((ny, cap, 128), BF16),
        ((nq, 256), F32), ((nx - 1, wide, 128), BF16), ((nx - 1, wide, 128), BF16),
        ((pairs, cap, 128), BF16), ((heads, cap, 128), BF16),
        ((pairs, long, 128), BF16), ((heads, long, 128), BF16),
        ((cap, width), BF16), ((cap, width), BF16),
        ((ny, HEAD_DIM, half), F32), ((ny, HEAD_DIM, half), BF16), ((ny, HEAD_DIM, half), BF16),
        ((ny, HEAD_DIM, half), BF16), ((ny - 1, HEAD_DIM, half), BF16),
        ((HEAD_DIM, half), F32),
        ((share * pairs, 16, 128), BF16), ((pairs - 1, share, 16, 128), BF16),
        ((share, 16, 128), F32), ((nx - 1, share, 16, 128), F32),
        ((share, 16, 128), BF16), ((pairs, share, 16, 128), BF16),
        ((HEAD_DIM, half), F32), ((3, rows, hd), BF16),
    ]
    zs, xs, ys, ps, one = dma((nz - 1,)), dma((nx - 1,)), dma((ny - 1,)), dma((pairs,)), dma
    scratch = [pltpu.VMEM(shape, kind) for shape, kind in buffers]
    scratch += [dma((5,)), dma((3,)), one, one, zs, zs]
    scratch += [zs, zs, zs, zs, xs, xs, ps, dma((ny,)), xs, xs, zs, zs]
    scratch += [one, one, ys, ys, dma((pairs - 1,)), dma((pairs - 1,)), xs, xs]
    scratch += [dma((sz.per_head,)), ps, dma((2 * ny - 1,)), dma((2,))]
    return pl.pallas_call(
        functools.partial(kernel, sz),
        out_shape=(grad, grad, grad, jax.ShapeDtypeStruct((sz.out_rows, width), F32)),
        in_specs=[vmem] + [hbm] * 5,
        out_specs=(hbm, hbm, hbm, vmem),
        scratch_shapes=scratch,
        compiler_params=pltpu.CompilerParams(
            collective_id=0, has_side_effects=True, vmem_limit_bytes=56 * 1024 * 1024
        ),
    )(visible, queries, keys, values, upstream, out_weight)


def build(mesh, nz, ny, cap):
    n_seq = mesh.shape["seq"]

    def run(queries, keys, values, upstream, out_weight, visible):
        hd, width = out_weight.shape
        sz = Sizes(n_seq // nz, nz, ny, queries.shape[1], cap, hd // HEAD_DIM, width)
        return per_device(sz, queries, keys, values, upstream, out_weight, visible)

    part = P("dp", "seq", None)
    return jax.shard_map(
        run,
        mesh=mesh,
        in_specs=(part, part, part, part, P(), P("dp", "seq")),
        out_specs=(part, part, part, P("seq", None)),
        check_vma=False,
    )


def solution(mesh):
    return build(mesh, Z_RING, Y_RING, VIS_MAX)
```

```python
import functools

import jax
import jax.numpy as jnp
from jax import lax
from jax.experimental import pallas as pl
from jax.experimental.pallas import tpu as pltpu
from jax.sharding import PartitionSpec as P

HEAD_DIM = 80
VIS_MAX = 144
Z_RING = 8
Y_RING = 4

BF16 = jnp.bfloat16
F32 = jnp.float32
MESH = pl.DeviceIdType.MESH
FAR = 1e30
DEAD = 64.0


def nn(a, b):
    return jnp.dot(a, b, preferred_element_type=F32)


def nt(a, b):
    return lax.dot_general(a, b, (((1,), (1,)), ((), ())), preferred_element_type=F32)


def identity(n):
    rows = lax.broadcasted_iota(jnp.int32, (n, n), 0)
    cols = lax.broadcasted_iota(jnp.int32, (n, n), 1)
    return jnp.where(rows == cols, 1.0, 0.0).astype(BF16)


def fold(tail):
    third = tail.shape[0] // 3
    parts = [tail[j * third : (j + 1) * third, :] for j in range(3)]
    return jnp.concatenate(parts + [jnp.zeros((third, 8), F32)], axis=1)


def unfold(folded):
    return jnp.concatenate([folded[:, 40 * j : 40 * j + 40] for j in range(3)], axis=0)


def lane_iota(rows, lanes):
    return lax.broadcasted_iota(jnp.int32, (rows, lanes), 1)


class Sizes:
    def __init__(self, nx, nz, ny, rows, cap, heads, width):
        self.nx, self.nz, self.ny = nx, nz, ny
        self.rows, self.cap, self.heads, self.width = rows, cap, heads, width
        self.pairs = nz // 2
        self.queries = self.pairs * cap
        self.keys = nx * self.queries
        self.hd = heads * HEAD_DIM
        self.half = width // 2
        self.col_tiles = self.half // 128
        self.tiles = (HEAD_DIM // 16) * self.col_tiles
        self.share = -(-self.tiles // self.pairs)
        self.out_rows = self.hd // (nx * nz)
        self.per_head = HEAD_DIM // self.out_rows


def kernel(
    sz,
    vis_ref, q_hbm, k_hbm, v_hbm, u_hbm, w_hbm,
    grads_hbm, gw_ref,
    qin, kin, vin, uin, win,
    send_a, recv_a, send_b, recv_b,
    send_g, recv_g, kv, kvt, q_mask, q_zero, d_out, scores,
    send_e, recv_e, dkv, send_c, recv_c, send_f, recv_f, send_d, recv_d,
    upk, upair, wown, wsend1, wrecv1, wsend2, wrecv2, red, tiles, wrecv3, wsend4, wrecv4, wsend5, wrecv5,
    full, stage,
    load_sem, store_sem, u_s, u_r, f_s, f_r,
    a_s, a_r, b_s, b_r, g_s, g_r, e_s, e_r, c_s, c_r, d_s, d_r,
    w1_s, w1_r, w2_s, w2_r, w3_s, w3_r, w4_s, w4_r, w5_s, w5_r, w6_s, w6_r,
):
    nx, nz, ny, cap, heads = sz.nx, sz.nz, sz.ny, sz.cap, sz.heads
    nq, half = sz.queries, sz.half
    scale = HEAD_DIM ** -0.5
    dp = lax.axis_index("dp")
    seq = lax.axis_index("seq")
    x, z = lax.div(seq, nz), lax.rem(seq, nz)
    y, core = lax.div(dp, 2), lax.rem(dp, 2)

    def z_peer(k):
        return lax.rem(z + k, nz)

    def x_peer(k):
        return lax.rem(x + k, nx)

    def at_z(k):
        return (dp, x * nz + z_peer(k))

    def at_x(k):
        return (dp, x_peer(k) * nz + z)

    def at_y(k):
        return (lax.rem(y + k, ny) * 2 + core, seq)

    def remote(src, dst, ss, rs, dev):
        return pltpu.make_async_remote_copy(
            src_ref=src, dst_ref=dst, send_sem=ss, recv_sem=rs, device_id=dev, device_id_type=MESH
        )

    barrier = pltpu.get_barrier_semaphore()
    peers = [at_z(k) for k in range(1, nz)] + [at_x(k) for k in range(1, nx)]
    peers += [(lax.rem(dp + k, 2 * ny), seq) for k in range(1, 2 * ny)]
    for peer in peers:
        pl.semaphore_signal(barrier, inc=1, device_id=peer, device_id_type=MESH)

    loads = []
    for i, (src, dst) in enumerate(
        [(v_hbm, vin), (k_hbm, kin), (q_hbm, qin), (u_hbm, uin), (w_hbm, win)]
    ):
        source = src.at[0] if i < 4 else src
        loads.append(pltpu.make_async_copy(source, dst, load_sem.at[i]))
        loads[-1].start()

    seen = vis_ref[...].astype(F32)
    rows = sz.rows
    upto = (
        lax.broadcasted_iota(jnp.int32, (rows, rows), 0)
        <= lax.broadcasted_iota(jnp.int32, (rows, rows), 1)
    )
    count = nn(jnp.broadcast_to(seen, (16, rows)).astype(BF16), jnp.where(upto, 1.0, 0.0).astype(BF16))
    rank = count[0:1, :].astype(jnp.int32) - 1
    odd = lax.rem(z, 2)
    slot = jnp.where(odd == 1, cap - 1 - rank, rank)
    slot = jnp.where(seen > 0.5, slot, -1)
    pick = jnp.where(lax.broadcasted_iota(jnp.int32, (cap, rows), 0) == slot, 1.0, 0.0)
    live = jnp.sum(pick, axis=1, keepdims=True)
    pick = pick.astype(BF16)

    loads[0].wait()
    loads[1].wait()
    pv, pk = nn(pick, vin[...]), nn(pick, kin[...])
    flags = jnp.broadcast_to(live, (cap, 8))

    def put(dst, h, left, right, extra):
        dst[h, 0:cap, :] = jnp.concatenate([left, right[:, 0:48]], axis=1).astype(BF16)
        dst[h, cap:, :] = fold(jnp.concatenate([right[:, 48:80], extra], axis=1)).astype(BF16)

    def head_cols(h):
        return slice(HEAD_DIM * h, HEAD_DIM * (h + 1))

    for h in range(heads):
        put(send_a, h, pv[:, head_cols(h)], pk[:, head_cols(h)], flags)

    pl.semaphore_wait(barrier, len(peers))

    def all_z(src, dst, ss, rs, start):
        copies = [remote(src(z_peer(k)), dst, ss.at[k - 1], rs.at[k - 1], at_z(k)) for k in range(1, nz)]
        if start:
            for copy in copies:
                copy.start()
        return copies

    a_copies = all_z(lambda t: send_a.at[t], recv_a.at[z], a_s, a_r, True)

    loads[2].wait()
    pq = nn(pick, qin[...])
    loads[3].wait()
    upk[...] = nn(pick, uin[...]).astype(BF16)
    loads[4].wait()
    for h in range(heads):
        part = nt(upk[...], win[HEAD_DIM * h : HEAD_DIM * (h + 1), :])
        put(send_b, h, pq[:, head_cols(h)], part, jnp.zeros((cap, 8), F32))

    recv_a[z] = send_a[z]
    recv_b[z] = send_b[z]
    eye = identity(256)
    unpick = nt(identity(rows), pick).astype(BF16)

    for copy in a_copies:
        copy.wait()
    base = pl.multiple_of(x * nq, 16)
    tails = []
    for p in range(sz.pairs):
        both = recv_a[2 * p].astype(F32) + recv_a[2 * p + 1].astype(F32)
        main, rest = both[0:cap, :], unfold(both[cap:, :])
        dead = rest[:, 32:33] < 0.5
        tails.append(rest[:, 0:32])
        mask = jnp.broadcast_to(jnp.where(dead, -1.0, 0.0), (cap, 96))
        kv[pl.ds(base + p * cap, cap), :] = jnp.concatenate([main, rest[:, 0:32], mask], axis=1).astype(BF16)
        marked = jnp.where(dead & (lane_iota(cap, 128) == 0), DEAD, main)
        send_g[p * cap : (p + 1) * cap, :] = marked.astype(BF16)
    send_g[nq:, 0 : 32 * sz.pairs] = jnp.concatenate(tails, axis=1).astype(BF16)
    g_copies = [
        remote(send_g, recv_g.at[k - 1], g_s.at[k - 1], g_r.at[k - 1], at_x(k)) for k in range(1, nx)
    ]
    for copy in g_copies:
        copy.start()
    b_copies = all_z(lambda t: send_b.at[t], recv_b.at[z], b_s, b_r, True)
    u_copy = remote(upk, upair, u_s, u_r, (dp, x * nz + lax.div(z, 2) * 2 + 1 - odd))
    for copy in b_copies:
        copy.wait()
    u_copy.start()
    for p in range(sz.pairs):
        both = recv_b[2 * p].astype(F32) + recv_b[2 * p + 1].astype(F32)
        main, rest = both[0:cap, :], unfold(both[cap:, :])
        at = slice(p * cap, (p + 1) * cap)
        query = jnp.concatenate(
            [jnp.zeros((cap, 80), F32), main[:, 0:80], jnp.zeros((cap, 96), F32)], axis=1
        )
        q_zero[at, :] = query.astype(BF16)
        q_mask[at, :] = jnp.where(lane_iota(cap, 256) == 240, FAR, query).astype(BF16)
        d_out[at, :] = jnp.concatenate(
            [main[:, 80:128], rest[:, 0:32], jnp.zeros((cap, 176), F32)], axis=1
        ).astype(BF16)

    def group(k):
        g = lax.rem(x + nx - k, nx)
        return g, pl.ds(pl.multiple_of(g * nq, 16), nq)

    def score_group(k, top):
        g, at = group(k)
        part = kv[at, :]
        value = nt(part, q_mask[...])
        scores[at, :] = value
        kvt[g] = nt(eye, part).astype(BF16)
        return jnp.maximum(top, jnp.max(value, axis=0, keepdims=True))

    top = score_group(0, jnp.full((1, nq), -3e38, F32))

    d_out_t = nt(eye[0:HEAD_DIM, 0:128], d_out[:, 0:128])

    for k in range(1, nx):
        g_copies[k - 1].wait()
        _, at = group(k)
        for p in range(sz.pairs):
            main = recv_g[k - 1, p * cap : (p + 1) * cap, :].astype(F32)
            rest = recv_g[k - 1, nq:, :].astype(F32)[:, 32 * p : 32 * p + 32]
            mask = jnp.broadcast_to(jnp.where(main[:, 0:1] > DEAD / 2, -1.0, 0.0), (cap, 96))
            start = pl.multiple_of(at.start + p * cap, 16)
            kv[pl.ds(start, cap), :] = jnp.concatenate([main, rest, mask], axis=1).astype(BF16)
        top = score_group(k, top)

    total = jnp.zeros((1, nq), F32)
    for k in range(nx):
        _, at = group(k)
        e = jnp.exp((scores[at, :] - top) * scale)
        scores[at, :] = e
        total = total + jnp.sum(e, axis=0, keepdims=True)
    inverse = 1.0 / total

    attended_t = jnp.zeros((HEAD_DIM, nq), F32)
    for k in range(nx):
        g, at = group(k)
        w = (scores[at, :] * inverse).astype(BF16)
        attended_t = attended_t + nn(kvt[g, 0:HEAD_DIM, :], w)
    attended_t = attended_t.astype(BF16)
    eye_q = identity(nq)
    send_e[...] = jnp.zeros_like(send_e)
    attended = nt(eye_q, attended_t).astype(BF16)
    for p in range(sz.pairs):
        send_e[p, :, 0:HEAD_DIM] = attended[p * cap : (p + 1) * cap, :]

    side = lax.div(z, ny)
    e_copies = []
    for p in range(sz.pairs):
        target = 2 * p + side
        copy = remote(
            send_e.at[p], recv_e.at[lax.rem(z, ny)], e_s.at[p], e_r.at[lax.rem(z, ny)], (dp, x * nz + target)
        )
        e_copies.append((copy, target != z))

        @pl.when(target != z)
        def _():
            copy.start()

        @pl.when(target == z)
        def _():
            recv_e[lax.rem(z, ny)] = send_e[p]

    delta = jnp.sum(d_out_t * attended_t.astype(F32), axis=0, keepdims=True)
    slope = inverse * scale

    dq_t = jnp.zeros((HEAD_DIM, nq), F32)
    c_copies = []
    for k in list(range(1, nx)) + [0]:
        g, at = group(k)
        e = scores[at, :]
        w = (e * inverse).astype(BF16)
        grad_prob = nt(kv[at, :], d_out[...])
        ds = (e * slope * (grad_prob - delta)).astype(BF16)
        term = nn(ds, q_zero[...]) + nn(w, d_out[...])
        if k == 0:
            dkv[...] = term
        else:
            send_c[k - 1, 0:nq, :] = term[:, 0:128].astype(BF16)
            send_c[k - 1, nq:, 0 : 32 * sz.pairs] = jnp.concatenate(
                [term[p * cap : (p + 1) * cap, 128:160] for p in range(sz.pairs)], axis=1
            ).astype(BF16)
            copy = remote(
                send_c.at[k - 1], recv_c.at[k - 1], c_s.at[k - 1], c_r.at[k - 1], (dp, g * nz + z)
            )
            copy.start()
            c_copies.append(copy)
        dq_t = dq_t + nn(kvt[g, HEAD_DIM : 2 * HEAD_DIM, :], ds)
    dq = nt(eye_q, dq_t.astype(BF16)).astype(BF16)
    send_f[...] = jnp.zeros_like(send_f)
    for p in range(sz.pairs):
        send_f[p, :, 0:HEAD_DIM] = dq[p * cap : (p + 1) * cap, :]
    f_copies = all_z(lambda t: send_f.at[lax.div(t, 2)], recv_f.at[z], f_s, f_r, True)
    recv_f[z] = send_f[lax.div(z, 2)]

    u_copy.wait()
    upk_all = (upk[...].astype(F32) + upair[...].astype(F32)).astype(BF16)
    upair[...] = upk_all
    for i in range(ny):
        source = odd * ny + i

        @pl.when(source != z)
        def _():
            remote(send_e.at[0], recv_e.at[i], e_s.at[0], e_r.at[i], (dp, x * nz + source)).wait_recv()

    for copy, away in e_copies:

        @pl.when(away)
        def _():
            copy.wait_send()

    terms = [nt(eye[0:128, 0:128], recv_e[i])[0:HEAD_DIM, :].astype(BF16) for i in range(ny)]
    other_cols = pl.ds(pl.multiple_of((1 - core) * half, 128), half)
    own_cols = pl.ds(pl.multiple_of(core * half, 128), half)
    for i in range(ny):
        wsend1[i] = nn(terms[i], upair[:, other_cols]).astype(BF16)
    w1 = remote(wsend1, wrecv1, w1_s, w1_r, (y * 2 + 1 - core, seq))
    w1.start()
    for i in range(ny):
        wown[i] = nn(terms[i], upair[:, own_cols])

    w1.wait()

    for i in range(ny):
        wown[i] = wown[i] + wrecv1[i].astype(F32)
        wsend2[i] = wown[i].astype(BF16)
    w2 = [
        remote(
            wsend2.at[lax.rem(y + k, ny)], wrecv2.at[k - 1], w2_s.at[k - 1], w2_r.at[k - 1], at_y(k)
        )
        for k in range(1, ny)
    ]
    for copy in w2:
        copy.start()

    for copy in w2:
        copy.wait()
    red[...] = wown[y]
    for k in range(1, ny):
        red[...] = red[...] + wrecv2[k - 1].astype(F32)
    tiles[...] = jnp.zeros_like(tiles)
    for r in range(HEAD_DIM // 16):
        for c in range(sz.col_tiles):
            tiles[r * sz.col_tiles + c] = red[16 * r : 16 * r + 16, 128 * c : 128 * c + 128].astype(BF16)
    share = sz.share
    w3 = [
        remote(
            tiles.at[pl.ds(lax.div(z_peer(2 * k), 2) * share, share)],
            wrecv3.at[k - 1], w3_s.at[k - 1], w3_r.at[k - 1], at_z(2 * k),
        )
        for k in range(1, sz.pairs)
    ]
    for copy in w3:
        copy.start()

    for copy in c_copies:
        copy.wait()
    mine, rest = dkv[:, 0:128], jnp.zeros((cap, 128), F32)
    for k in range(1, nx):
        mine = mine + recv_c[k - 1, 0:nq, :].astype(F32)
        rest = rest + recv_c[k - 1, nq:, :].astype(F32)
    for p in range(sz.pairs):
        at = slice(p * cap, (p + 1) * cap)
        tail = dkv[at, 128:160] + rest[:, 32 * p : 32 * p + 32]
        send_d[p, 0:cap, :] = mine[at, :].astype(BF16)
        send_d[p, cap:, :] = fold(jnp.concatenate([tail, jnp.zeros((cap, 8), F32)], axis=1)).astype(BF16)
    d_copies = all_z(lambda t: send_d.at[lax.div(t, 2)], recv_d.at[z], d_s, d_r, True)
    recv_d[z] = send_d[lax.div(z, 2)]

    stores = []

    def give(t, dst, parts):
        merged = jnp.concatenate(parts, axis=1).astype(BF16)
        stage[t] = nn(unpick, merged).astype(BF16)
        stores.append(pltpu.make_async_copy(stage.at[t], dst, store_sem.at[t]))
        stores[-1].start()

    for copy in w3:
        copy.wait()
    part = tiles[pl.ds(lax.div(z, 2) * share, share)].astype(F32)
    for k in range(1, sz.pairs):
        part = part + wrecv3[k - 1].astype(F32)
    wsend4[...] = part
    per_head, out_rows = sz.per_head, sz.out_rows
    head = odd * ny + y
    row = lax.div(head * per_head, nz)
    w4 = [
        remote(wsend4, wrecv4.at[k - 1], w4_s.at[k - 1], w4_r.at[k - 1], at_x(k)) for k in range(1, nx)
    ]
    for k in range(1, nx):

        @pl.when(x_peer(k) == row)
        def _():
            w4[k - 1].start()

    first = lax.rem(head * per_head, nz)
    w5 = [
        remote(
            wsend5, wrecv5.at[lax.div(z, 2)], w5_s.at[q], w5_r.at[lax.div(z, 2)], (dp, x * nz + first + q)
        )
        for q in range(per_head)
    ]

    @pl.when(x == row)
    def _():
        for copy in w4:
            copy.wait_recv()
        summed = wsend4[...]
        for k in range(1, nx):
            summed = summed + wrecv4[k - 1]
        wsend5[...] = summed.astype(BF16)
        for q in range(per_head):

            @pl.when(first + q != z)
            def _():
                w5[q].start()

            @pl.when(first + q == z)
            def _():
                wrecv5[lax.div(z, 2)] = wsend5[...]

    for copy in f_copies:
        copy.wait()
    give(0, grads_hbm.at[0], [recv_f[h].astype(F32)[:, 0:HEAD_DIM] for h in range(heads)])

    block = lax.div(seq, per_head)
    owner = y == lax.rem(block, ny)
    w6 = [
        remote(
            gw_ref.at[:, own_cols], gw_ref.at[:, own_cols], w6_s.at[k - 1], w6_r.at[core],
            (lax.rem(dp + k, 2 * ny), seq),
        )
        for k in range(1, 2 * ny)
    ]
    w6_other = remote(
        gw_ref.at[:, other_cols], gw_ref.at[:, other_cols], w6_s.at[0], w6_r.at[1 - core],
        (y * 2 + 1 - core, seq),
    )

    @pl.when(owner)
    def _():
        for j in range(sz.pairs):
            source = 2 * j + lax.div(block, ny)

            @pl.when(source != z)
            def _():
                remote(
                    wsend5, wrecv5.at[j], w5_s.at[0], w5_r.at[j], (dp, x * nz + source)
                ).wait_recv()

        for r in range(HEAD_DIM // 16):
            for c in range(sz.col_tiles):
                t = r * sz.col_tiles + c
                full[16 * r : 16 * r + 16, 128 * c : 128 * c + 128] = wrecv5[t // share, t % share].astype(F32)
        for q in range(per_head):

            @pl.when(lax.rem(seq, per_head) == q)
            def _():
                gw_ref[:, own_cols] = full[out_rows * q : out_rows * (q + 1), :]

        for copy in w6:
            copy.start()

    for copy in d_copies:
        copy.wait()
    give(1, grads_hbm.at[2], [recv_d[h, 0:cap, :].astype(F32)[:, 0:HEAD_DIM] for h in range(heads)])

    keys_parts = []
    for h in range(heads):
        keys_parts.append(recv_d[h, 0:cap, :].astype(F32)[:, HEAD_DIM:])
        keys_parts.append(unfold(recv_d[h, cap:, :].astype(F32))[:, 0:32])
    give(2, grads_hbm.at[1], keys_parts)

    @pl.when(jnp.logical_not(owner))
    def _():
        w6[0].wait_recv()

    w6_other.wait_recv()

    @pl.when(owner)
    def _():
        for copy in w6:
            copy.wait_send()

    @pl.when(x == row)
    def _():
        for q in range(per_head):

            @pl.when(first + q != z)
            def _():
                w5[q].wait_send()

    for k in range(1, nx):

        @pl.when(x_peer(k) == row)
        def _():
            w4[k - 1].wait_send()

    for copy in stores:
        copy.wait()


def per_device(sz, queries, keys, values, upstream, out_weight, visible):
    nx, nz, ny, cap, heads = sz.nx, sz.nz, sz.ny, sz.cap, sz.heads
    nq, nk, hd, width, rows = sz.queries, sz.keys, sz.hd, sz.width, sz.rows
    half, share, pairs = sz.half, sz.share, sz.pairs
    long, wide = cap + cap // 3, nq + cap
    hbm = pl.BlockSpec(memory_space=pl.ANY)
    vmem = pl.BlockSpec(memory_space=pltpu.VMEM)
    grad = jax.ShapeDtypeStruct((3, rows, hd), BF16)
    dma = pltpu.SemaphoreType.DMA
    buffers = [
        ((rows, hd), BF16), ((rows, hd), BF16), ((rows, hd), BF16), ((rows, width), BF16), ((hd, width), BF16),
        ((heads, long, 128), BF16), ((heads, long, 128), BF16),
        ((heads, long, 128), BF16), ((heads, long, 128), BF16),
        ((wide, 128), BF16), ((nx - 1, wide, 128), BF16),
        ((nk, 256), BF16), ((nx, 256, nq), BF16), ((nq, 256), BF16), ((nq, 256), BF16), ((nq, 256), BF16),
        ((nk, nq), F32),
        ((pairs, cap, 128), BF16), ((ny, cap, 128), BF16),
        ((nq, 256), F32), ((nx - 1, wide, 128), BF16), ((nx - 1, wide, 128), BF16),
        ((pairs, cap, 128), BF16), ((heads, cap, 128), BF16),
        ((pairs, long, 128), BF16), ((heads, long, 128), BF16),
        ((cap, width), BF16), ((cap, width), BF16),
        ((ny, HEAD_DIM, half), F32), ((ny, HEAD_DIM, half), BF16), ((ny, HEAD_DIM, half), BF16),
        ((ny, HEAD_DIM, half), BF16), ((ny - 1, HEAD_DIM, half), BF16),
        ((HEAD_DIM, half), F32),
        ((share * pairs, 16, 128), BF16), ((pairs - 1, share, 16, 128), BF16),
        ((share, 16, 128), F32), ((nx - 1, share, 16, 128), F32),
        ((share, 16, 128), BF16), ((pairs, share, 16, 128), BF16),
        ((HEAD_DIM, half), F32), ((3, rows, hd), BF16),
    ]
    zs, xs, ys, ps, one = dma((nz - 1,)), dma((nx - 1,)), dma((ny - 1,)), dma((pairs,)), dma
    scratch = [pltpu.VMEM(shape, kind) for shape, kind in buffers]
    scratch += [dma((5,)), dma((3,)), one, one, zs, zs]
    scratch += [zs, zs, zs, zs, xs, xs, ps, dma((ny,)), xs, xs, zs, zs]
    scratch += [one, one, ys, ys, dma((pairs - 1,)), dma((pairs - 1,)), xs, xs]
    scratch += [dma((sz.per_head,)), ps, dma((2 * ny - 1,)), dma((2,))]
    grads, weight = pl.pallas_call(
        functools.partial(kernel, sz),
        out_shape=(grad, jax.ShapeDtypeStruct((sz.out_rows, width), F32)),
        in_specs=[vmem] + [hbm] * 5,
        out_specs=(hbm, vmem),
        scratch_shapes=scratch,
        compiler_params=pltpu.CompilerParams(
            collective_id=0, has_side_effects=True, vmem_limit_bytes=56 * 1024 * 1024
        ),
    )(visible, queries, keys, values, upstream, out_weight)
    return grads[0:1], grads[1:2], grads[2:3], weight


def build(mesh, nz, ny, cap):
    n_seq = mesh.shape["seq"]

    def run(queries, keys, values, upstream, out_weight, visible):
        hd, width = out_weight.shape
        sz = Sizes(n_seq // nz, nz, ny, queries.shape[1], cap, hd // HEAD_DIM, width)
        return per_device(sz, queries, keys, values, upstream, out_weight, visible)

    part = P("dp", "seq", None)
    return jax.shard_map(
        run,
        mesh=mesh,
        in_specs=(part, part, part, part, P(), P("dp", "seq")),
        out_specs=(part, part, part, P("seq", None)),
        check_vma=False,
    )


def solution(mesh):
    return build(mesh, Z_RING, Y_RING, VIS_MAX)
```

```python
import functools

import jax
import jax.numpy as jnp
from jax import lax
from jax.experimental import pallas as pl
from jax.experimental.pallas import tpu as pltpu
from jax.sharding import PartitionSpec as P

HEAD_DIM = 80
VIS_MAX = 144
Z_RING = 8
Y_RING = 4

BF16 = jnp.bfloat16
F32 = jnp.float32
MESH = pl.DeviceIdType.MESH
FAR = 1e30
DEAD = 64.0


def nn(a, b):
    return jnp.dot(a, b, preferred_element_type=F32)


def nt(a, b):
    return lax.dot_general(a, b, (((1,), (1,)), ((), ())), preferred_element_type=F32)


def identity(n):
    rows = lax.broadcasted_iota(jnp.int32, (n, n), 0)
    cols = lax.broadcasted_iota(jnp.int32, (n, n), 1)
    return jnp.where(rows == cols, 1.0, 0.0).astype(BF16)


def fold(tail):
    third = tail.shape[0] // 3
    parts = [tail[j * third : (j + 1) * third, :] for j in range(3)]
    return jnp.concatenate(parts + [jnp.zeros((third, 8), F32)], axis=1)


def unfold(folded):
    return jnp.concatenate([folded[:, 40 * j : 40 * j + 40] for j in range(3)], axis=0)


def lane_iota(rows, lanes):
    return lax.broadcasted_iota(jnp.int32, (rows, lanes), 1)


class Sizes:
    def __init__(self, nx, nz, ny, rows, cap, heads, width):
        self.nx, self.nz, self.ny = nx, nz, ny
        self.rows, self.cap, self.heads, self.width = rows, cap, heads, width
        self.pairs = nz // 2
        self.queries = self.pairs * cap
        self.keys = nx * self.queries
        self.hd = heads * HEAD_DIM
        self.half = width // 2
        self.col_tiles = self.half // 128
        self.tiles = (HEAD_DIM // 16) * self.col_tiles
        self.share = -(-self.tiles // self.pairs)
        self.out_rows = self.hd // (nx * nz)
        self.per_head = HEAD_DIM // self.out_rows


def kernel(
    sz,
    vis_ref, q_hbm, k_hbm, v_hbm, u_hbm, w_hbm,
    grads_hbm, gw_ref,
    qin, kin, vin, uin, win,
    send_a, recv_a, send_b, recv_b,
    send_g, recv_g, kv, kvt, q_mask, q_zero, d_out, scores,
    send_e, recv_e, dkv, send_c, recv_c, send_f, recv_f, send_d, recv_d,
    upk, upair, wown, wsend1, wrecv1, wsend2, wrecv2, red, tiles, wrecv3, wsend4, wrecv4, wsend5, wrecv5,
    full, stage,
    load_sem, store_sem, u_s, u_r, f_s, f_r,
    a_s, a_r, b_s, b_r, g_s, g_r, e_s, e_r, c_s, c_r, d_s, d_r,
    w1_s, w1_r, w2_s, w2_r, w3_s, w3_r, w4_s, w4_r, w5_s, w5_r, w6_s, w6_r,
):
    nx, nz, ny, cap, heads = sz.nx, sz.nz, sz.ny, sz.cap, sz.heads
    nq, half = sz.queries, sz.half
    scale = HEAD_DIM ** -0.5
    dp = lax.axis_index("dp")
    seq = lax.axis_index("seq")
    x, z = lax.div(seq, nz), lax.rem(seq, nz)
    y, core = lax.div(dp, 2), lax.rem(dp, 2)

    def z_peer(k):
        return lax.rem(z + k, nz)

    def x_peer(k):
        return lax.rem(x + k, nx)

    def at_z(k):
        return (dp, x * nz + z_peer(k))

    def at_x(k):
        return (dp, x_peer(k) * nz + z)

    def at_y(k):
        return (lax.rem(y + k, ny) * 2 + core, seq)

    def remote(src, dst, ss, rs, dev):
        return pltpu.make_async_remote_copy(
            src_ref=src, dst_ref=dst, send_sem=ss, recv_sem=rs, device_id=dev, device_id_type=MESH
        )

    barrier = pltpu.get_barrier_semaphore()
    peers = [at_z(k) for k in range(1, nz)] + [at_x(k) for k in range(1, nx)]
    peers += [(lax.rem(dp + k, 2 * ny), seq) for k in range(1, 2 * ny)]
    for peer in peers:
        pl.semaphore_signal(barrier, inc=1, device_id=peer, device_id_type=MESH)

    loads = []
    for i, (src, dst) in enumerate(
        [(v_hbm, vin), (k_hbm, kin), (q_hbm, qin), (u_hbm, uin), (w_hbm, win)]
    ):
        source = src.at[0] if i < 4 else src
        loads.append(pltpu.make_async_copy(source, dst, load_sem.at[i]))
        if i < 2:
            loads[-1].start()

    seen = vis_ref[...].astype(F32)
    rows = sz.rows
    upto = (
        lax.broadcasted_iota(jnp.int32, (rows, rows), 0)
        <= lax.broadcasted_iota(jnp.int32, (rows, rows), 1)
    )
    count = nn(jnp.broadcast_to(seen, (16, rows)).astype(BF16), jnp.where(upto, 1.0, 0.0).astype(BF16))
    rank = count[0:1, :].astype(jnp.int32) - 1
    odd = lax.rem(z, 2)
    slot = jnp.where(odd == 1, cap - 1 - rank, rank)
    slot = jnp.where(seen > 0.5, slot, -1)
    pick = jnp.where(lax.broadcasted_iota(jnp.int32, (cap, rows), 0) == slot, 1.0, 0.0)
    live = jnp.sum(pick, axis=1, keepdims=True)
    pick = pick.astype(BF16)

    loads[0].wait()
    loads[1].wait()
    for load in loads[2:]:
        load.start()
    pv, pk = nn(pick, vin[...]), nn(pick, kin[...])
    flags = jnp.broadcast_to(live, (cap, 8))

    def put(dst, h, left, right, extra):
        dst[h, 0:cap, :] = jnp.concatenate([left, right[:, 0:48]], axis=1).astype(BF16)
        dst[h, cap:, :] = fold(jnp.concatenate([right[:, 48:80], extra], axis=1)).astype(BF16)

    def head_cols(h):
        return slice(HEAD_DIM * h, HEAD_DIM * (h + 1))

    for h in range(heads):
        put(send_a, h, pv[:, head_cols(h)], pk[:, head_cols(h)], flags)

    pl.semaphore_wait(barrier, len(peers))

    def all_z(src, dst, ss, rs, start):
        copies = [remote(src(z_peer(k)), dst, ss.at[k - 1], rs.at[k - 1], at_z(k)) for k in range(1, nz)]
        if start:
            for copy in copies:
                copy.start()
        return copies

    a_copies = all_z(lambda t: send_a.at[t], recv_a.at[z], a_s, a_r, True)

    loads[2].wait()
    pq = nn(pick, qin[...])
    loads[3].wait()
    upk[...] = nn(pick, uin[...]).astype(BF16)
    loads[4].wait()
    for h in range(heads):
        part = nt(upk[...], win[HEAD_DIM * h : HEAD_DIM * (h + 1), :])
        put(send_b, h, pq[:, head_cols(h)], part, jnp.zeros((cap, 8), F32))

    recv_a[z] = send_a[z]
    recv_b[z] = send_b[z]
    eye = identity(256)
    eye_q = identity(nq)
    send_e[...] = jnp.zeros_like(send_e)
    send_f[...] = jnp.zeros_like(send_f)
    tiles[...] = jnp.zeros_like(tiles)
    unpick = nt(identity(rows), pick).astype(BF16)

    for copy in a_copies:
        copy.wait()
    base = pl.multiple_of(x * nq, 16)
    tails = []
    for p in range(sz.pairs):
        both = recv_a[2 * p].astype(F32) + recv_a[2 * p + 1].astype(F32)
        main, rest = both[0:cap, :], unfold(both[cap:, :])
        dead = rest[:, 32:33] < 0.5
        tails.append(rest[:, 0:32])
        mask = jnp.broadcast_to(jnp.where(dead, -1.0, 0.0), (cap, 96))
        kv[pl.ds(base + p * cap, cap), :] = jnp.concatenate([main, rest[:, 0:32], mask], axis=1).astype(BF16)
        marked = jnp.where(dead & (lane_iota(cap, 128) == 0), DEAD, main)
        send_g[p * cap : (p + 1) * cap, :] = marked.astype(BF16)
    send_g[nq:, 0 : 32 * sz.pairs] = jnp.concatenate(tails, axis=1).astype(BF16)
    g_copies = [
        remote(send_g, recv_g.at[k - 1], g_s.at[k - 1], g_r.at[k - 1], at_x(k)) for k in range(1, nx)
    ]
    for copy in g_copies:
        copy.start()
    b_copies = all_z(lambda t: send_b.at[t], recv_b.at[z], b_s, b_r, True)
    u_copy = remote(upk, upair, u_s, u_r, (dp, x * nz + lax.div(z, 2) * 2 + 1 - odd))
    for copy in b_copies:
        copy.wait()
    u_copy.start()
    for p in range(sz.pairs):
        both = recv_b[2 * p].astype(F32) + recv_b[2 * p + 1].astype(F32)
        main, rest = both[0:cap, :], unfold(both[cap:, :])
        at = slice(p * cap, (p + 1) * cap)
        query = jnp.concatenate(
            [jnp.zeros((cap, 80), F32), main[:, 0:80], jnp.zeros((cap, 96), F32)], axis=1
        )
        q_zero[at, :] = query.astype(BF16)
        q_mask[at, :] = jnp.where(lane_iota(cap, 256) == 240, FAR, query).astype(BF16)
        d_out[at, :] = jnp.concatenate(
            [main[:, 80:128], rest[:, 0:32], jnp.zeros((cap, 176), F32)], axis=1
        ).astype(BF16)

    def group(k):
        g = lax.rem(x + nx - k, nx)
        return g, pl.ds(pl.multiple_of(g * nq, 16), nq)

    def score_group(k, top):
        g, at = group(k)
        part = kv[at, :]
        value = nt(part, q_mask[...])
        scores[at, :] = value
        kvt[g] = nt(eye, part).astype(BF16)
        return jnp.maximum(top, jnp.max(value, axis=0, keepdims=True))

    top = score_group(0, jnp.full((1, nq), -3e38, F32))

    d_out_t = nt(eye[0:HEAD_DIM, 0:128], d_out[:, 0:128])

    for k in range(1, nx):
        g_copies[k - 1].wait()
        _, at = group(k)
        for p in range(sz.pairs):
            main = recv_g[k - 1, p * cap : (p + 1) * cap, :].astype(F32)
            rest = recv_g[k - 1, nq:, :].astype(F32)[:, 32 * p : 32 * p + 32]
            mask = jnp.broadcast_to(jnp.where(main[:, 0:1] > DEAD / 2, -1.0, 0.0), (cap, 96))
            start = pl.multiple_of(at.start + p * cap, 16)
            kv[pl.ds(start, cap), :] = jnp.concatenate([main, rest, mask], axis=1).astype(BF16)
        top = score_group(k, top)

    total = jnp.zeros((1, nq), F32)
    for k in range(nx):
        _, at = group(k)
        e = jnp.exp((scores[at, :] - top) * scale)
        scores[at, :] = e
        total = total + jnp.sum(e, axis=0, keepdims=True)
    inverse = 1.0 / total

    attended_t = jnp.zeros((HEAD_DIM, nq), F32)
    for k in range(nx):
        g, at = group(k)
        w = (scores[at, :] * inverse).astype(BF16)
        attended_t = attended_t + nn(kvt[g, 0:HEAD_DIM, :], w)
    attended_t = attended_t.astype(BF16)
    attended = nt(eye_q, attended_t).astype(BF16)
    for p in range(sz.pairs):
        send_e[p, :, 0:HEAD_DIM] = attended[p * cap : (p + 1) * cap, :]

    side = lax.div(z, ny)
    e_copies = []
    for p in range(sz.pairs):
        target = 2 * p + side
        copy = remote(
            send_e.at[p], recv_e.at[lax.rem(z, ny)], e_s.at[p], e_r.at[lax.rem(z, ny)], (dp, x * nz + target)
        )
        e_copies.append((copy, target != z))

        @pl.when(target != z)
        def _():
            copy.start()

        @pl.when(target == z)
        def _():
            recv_e[lax.rem(z, ny)] = send_e[p]

    delta = jnp.sum(d_out_t * attended_t.astype(F32), axis=0, keepdims=True)
    slope = inverse * scale

    dq_t = jnp.zeros((HEAD_DIM, nq), F32)
    c_copies = []
    for k in list(range(1, nx)) + [0]:
        g, at = group(k)
        e = scores[at, :]
        w = (e * inverse).astype(BF16)
        grad_prob = nt(kv[at, :], d_out[...])
        ds = (e * slope * (grad_prob - delta)).astype(BF16)
        term = nn(ds, q_zero[...]) + nn(w, d_out[...])
        if k == 0:
            dkv[...] = term
        else:
            send_c[k - 1, 0:nq, :] = term[:, 0:128].astype(BF16)
            send_c[k - 1, nq:, 0 : 32 * sz.pairs] = jnp.concatenate(
                [term[p * cap : (p + 1) * cap, 128:160] for p in range(sz.pairs)], axis=1
            ).astype(BF16)
            copy = remote(
                send_c.at[k - 1], recv_c.at[k - 1], c_s.at[k - 1], c_r.at[k - 1], (dp, g * nz + z)
            )
            copy.start()
            c_copies.append(copy)
        dq_t = dq_t + nn(kvt[g, HEAD_DIM : 2 * HEAD_DIM, :], ds)
    dq = nt(eye_q, dq_t.astype(BF16)).astype(BF16)
    for p in range(sz.pairs):
        send_f[p, :, 0:HEAD_DIM] = dq[p * cap : (p + 1) * cap, :]
    f_copies = all_z(lambda t: send_f.at[lax.div(t, 2)], recv_f.at[z], f_s, f_r, True)
    recv_f[z] = send_f[lax.div(z, 2)]

    u_copy.wait()
    upk_all = (upk[...].astype(F32) + upair[...].astype(F32)).astype(BF16)
    upair[...] = upk_all
    for i in range(ny):
        source = odd * ny + i

        @pl.when(source != z)
        def _():
            remote(send_e.at[0], recv_e.at[i], e_s.at[0], e_r.at[i], (dp, x * nz + source)).wait_recv()

    for copy, away in e_copies:

        @pl.when(away)
        def _():
            copy.wait_send()

    terms = [nt(eye[0:128, 0:128], recv_e[i])[0:HEAD_DIM, :].astype(BF16) for i in range(ny)]
    other_cols = pl.ds(pl.multiple_of((1 - core) * half, 128), half)
    own_cols = pl.ds(pl.multiple_of(core * half, 128), half)
    for i in range(ny):
        wsend1[i] = nn(terms[i], upair[:, other_cols]).astype(BF16)
    w1 = remote(wsend1, wrecv1, w1_s, w1_r, (y * 2 + 1 - core, seq))
    w1.start()
    for i in range(ny):
        wown[i] = nn(terms[i], upair[:, own_cols])

    w1.wait()

    for i in range(ny):
        wown[i] = wown[i] + wrecv1[i].astype(F32)
        wsend2[i] = wown[i].astype(BF16)
    w2 = [
        remote(
            wsend2.at[lax.rem(y + k, ny)], wrecv2.at[k - 1], w2_s.at[k - 1], w2_r.at[k - 1], at_y(k)
        )
        for k in range(1, ny)
    ]
    for copy in w2:
        copy.start()

    for copy in w2:
        copy.wait()
    red[...] = wown[y]
    for k in range(1, ny):
        red[...] = red[...] + wrecv2[k - 1].astype(F32)
    for r in range(HEAD_DIM // 16):
        for c in range(sz.col_tiles):
            tiles[r * sz.col_tiles + c] = red[16 * r : 16 * r + 16, 128 * c : 128 * c + 128].astype(BF16)
    share = sz.share
    w3 = [
        remote(
            tiles.at[pl.ds(lax.div(z_peer(2 * k), 2) * share, share)],
            wrecv3.at[k - 1], w3_s.at[k - 1], w3_r.at[k - 1], at_z(2 * k),
        )
        for k in range(1, sz.pairs)
    ]
    for copy in w3:
        copy.start()

    for copy in c_copies:
        copy.wait()
    mine, rest = dkv[:, 0:128], jnp.zeros((cap, 128), F32)
    for k in range(1, nx):
        mine = mine + recv_c[k - 1, 0:nq, :].astype(F32)
        rest = rest + recv_c[k - 1, nq:, :].astype(F32)
    for p in range(sz.pairs):
        at = slice(p * cap, (p + 1) * cap)
        tail = dkv[at, 128:160] + rest[:, 32 * p : 32 * p + 32]
        send_d[p, 0:cap, :] = mine[at, :].astype(BF16)
        send_d[p, cap:, :] = fold(jnp.concatenate([tail, jnp.zeros((cap, 8), F32)], axis=1)).astype(BF16)
    d_copies = all_z(lambda t: send_d.at[lax.div(t, 2)], recv_d.at[z], d_s, d_r, True)
    recv_d[z] = send_d[lax.div(z, 2)]

    stores = []

    def give(t, dst, parts):
        merged = jnp.concatenate(parts, axis=1).astype(BF16)
        stage[t] = nn(unpick, merged).astype(BF16)
        stores.append(pltpu.make_async_copy(stage.at[t], dst, store_sem.at[t]))
        stores[-1].start()

    for copy in w3:
        copy.wait()
    part = tiles[pl.ds(lax.div(z, 2) * share, share)].astype(F32)
    for k in range(1, sz.pairs):
        part = part + wrecv3[k - 1].astype(F32)
    wsend4[...] = part
    per_head, out_rows = sz.per_head, sz.out_rows
    head = odd * ny + y
    row = lax.div(head * per_head, nz)
    w4 = [
        remote(wsend4, wrecv4.at[k - 1], w4_s.at[k - 1], w4_r.at[k - 1], at_x(k)) for k in range(1, nx)
    ]
    for k in range(1, nx):

        @pl.when(x_peer(k) == row)
        def _():
            w4[k - 1].start()

    first = lax.rem(head * per_head, nz)
    w5 = [
        remote(
            wsend5, wrecv5.at[lax.div(z, 2)], w5_s.at[q], w5_r.at[lax.div(z, 2)], (dp, x * nz + first + q)
        )
        for q in range(per_head)
    ]

    @pl.when(x == row)
    def _():
        for copy in w4:
            copy.wait_recv()
        summed = wsend4[...]
        for k in range(1, nx):
            summed = summed + wrecv4[k - 1]
        wsend5[...] = summed.astype(BF16)
        for q in range(per_head):

            @pl.when(first + q != z)
            def _():
                w5[q].start()

            @pl.when(first + q == z)
            def _():
                wrecv5[lax.div(z, 2)] = wsend5[...]

    for copy in f_copies:
        copy.wait()
    give(0, grads_hbm.at[0], [recv_f[h].astype(F32)[:, 0:HEAD_DIM] for h in range(heads)])

    block = lax.div(seq, per_head)
    owner = y == lax.rem(block, ny)
    w6 = [
        remote(
            gw_ref.at[:, own_cols], gw_ref.at[:, own_cols], w6_s.at[k - 1], w6_r.at[core],
            (lax.rem(dp + k, 2 * ny), seq),
        )
        for k in range(1, 2 * ny)
    ]
    w6_other = remote(
        gw_ref.at[:, other_cols], gw_ref.at[:, other_cols], w6_s.at[0], w6_r.at[1 - core],
        (y * 2 + 1 - core, seq),
    )

    @pl.when(owner)
    def _():
        for j in range(sz.pairs):
            source = 2 * j + lax.div(block, ny)

            @pl.when(source != z)
            def _():
                remote(
                    wsend5, wrecv5.at[j], w5_s.at[0], w5_r.at[j], (dp, x * nz + source)
                ).wait_recv()

        for r in range(HEAD_DIM // 16):
            for c in range(sz.col_tiles):
                t = r * sz.col_tiles + c
                full[16 * r : 16 * r + 16, 128 * c : 128 * c + 128] = wrecv5[t // share, t % share].astype(F32)
        for q in range(per_head):

            @pl.when(lax.rem(seq, per_head) == q)
            def _():
                gw_ref[:, own_cols] = full[out_rows * q : out_rows * (q + 1), :]

        for copy in w6:
            copy.start()

    for copy in d_copies:
        copy.wait()
    give(1, grads_hbm.at[2], [recv_d[h, 0:cap, :].astype(F32)[:, 0:HEAD_DIM] for h in range(heads)])

    keys_parts = []
    for h in range(heads):
        keys_parts.append(recv_d[h, 0:cap, :].astype(F32)[:, HEAD_DIM:])
        keys_parts.append(unfold(recv_d[h, cap:, :].astype(F32))[:, 0:32])
    give(2, grads_hbm.at[1], keys_parts)

    @pl.when(jnp.logical_not(owner))
    def _():
        w6[0].wait_recv()

    w6_other.wait_recv()

    @pl.when(owner)
    def _():
        for copy in w6:
            copy.wait_send()

    @pl.when(x == row)
    def _():
        for q in range(per_head):

            @pl.when(first + q != z)
            def _():
                w5[q].wait_send()

    for k in range(1, nx):

        @pl.when(x_peer(k) == row)
        def _():
            w4[k - 1].wait_send()

    for copy in stores:
        copy.wait()


def per_device(sz, queries, keys, values, upstream, out_weight, visible):
    nx, nz, ny, cap, heads = sz.nx, sz.nz, sz.ny, sz.cap, sz.heads
    nq, nk, hd, width, rows = sz.queries, sz.keys, sz.hd, sz.width, sz.rows
    half, share, pairs = sz.half, sz.share, sz.pairs
    long, wide = cap + cap // 3, nq + cap
    hbm = pl.BlockSpec(memory_space=pl.ANY)
    vmem = pl.BlockSpec(memory_space=pltpu.VMEM)
    grad = jax.ShapeDtypeStruct((3, rows, hd), BF16)
    dma = pltpu.SemaphoreType.DMA
    buffers = [
        ((rows, hd), BF16), ((rows, hd), BF16), ((rows, hd), BF16), ((rows, width), BF16), ((hd, width), BF16),
        ((heads, long, 128), BF16), ((heads, long, 128), BF16),
        ((heads, long, 128), BF16), ((heads, long, 128), BF16),
        ((wide, 128), BF16), ((nx - 1, wide, 128), BF16),
        ((nk, 256), BF16), ((nx, 256, nq), BF16), ((nq, 256), BF16), ((nq, 256), BF16), ((nq, 256), BF16),
        ((nk, nq), F32),
        ((pairs, cap, 128), BF16), ((ny, cap, 128), BF16),
        ((nq, 256), F32), ((nx - 1, wide, 128), BF16), ((nx - 1, wide, 128), BF16),
        ((pairs, cap, 128), BF16), ((heads, cap, 128), BF16),
        ((pairs, long, 128), BF16), ((heads, long, 128), BF16),
        ((cap, width), BF16), ((cap, width), BF16),
        ((ny, HEAD_DIM, half), F32), ((ny, HEAD_DIM, half), BF16), ((ny, HEAD_DIM, half), BF16),
        ((ny, HEAD_DIM, half), BF16), ((ny - 1, HEAD_DIM, half), BF16),
        ((HEAD_DIM, half), F32),
        ((share * pairs, 16, 128), BF16), ((pairs - 1, share, 16, 128), BF16),
        ((share, 16, 128), F32), ((nx - 1, share, 16, 128), F32),
        ((share, 16, 128), BF16), ((pairs, share, 16, 128), BF16),
        ((HEAD_DIM, half), F32), ((3, rows, hd), BF16),
    ]
    zs, xs, ys, ps, one = dma((nz - 1,)), dma((nx - 1,)), dma((ny - 1,)), dma((pairs,)), dma
    scratch = [pltpu.VMEM(shape, kind) for shape, kind in buffers]
    scratch += [dma((5,)), dma((3,)), one, one, zs, zs]
    scratch += [zs, zs, zs, zs, xs, xs, ps, dma((ny,)), xs, xs, zs, zs]
    scratch += [one, one, ys, ys, dma((pairs - 1,)), dma((pairs - 1,)), xs, xs]
    scratch += [dma((sz.per_head,)), ps, dma((2 * ny - 1,)), dma((2,))]
    grads, weight = pl.pallas_call(
        functools.partial(kernel, sz),
        out_shape=(grad, jax.ShapeDtypeStruct((sz.out_rows, width), F32)),
        in_specs=[vmem] + [hbm] * 5,
        out_specs=(hbm, vmem),
        scratch_shapes=scratch,
        compiler_params=pltpu.CompilerParams(
            collective_id=0, has_side_effects=True, vmem_limit_bytes=56 * 1024 * 1024
        ),
    )(visible, queries, keys, values, upstream, out_weight)
    return grads[0:1], grads[1:2], grads[2:3], weight


def build(mesh, nz, ny, cap):
    n_seq = mesh.shape["seq"]

    def run(queries, keys, values, upstream, out_weight, visible):
        hd, width = out_weight.shape
        sz = Sizes(n_seq // nz, nz, ny, queries.shape[1], cap, hd // HEAD_DIM, width)
        return per_device(sz, queries, keys, values, upstream, out_weight, visible)

    part = P("dp", "seq", None)
    return jax.shard_map(
        run,
        mesh=mesh,
        in_specs=(part, part, part, part, P(), P("dp", "seq")),
        out_specs=(part, part, part, P("seq", None)),
        check_vma=False,
    )


def solution(mesh):
    return build(mesh, Z_RING, Y_RING, VIS_MAX)
```
